256 devices in a mesh: ctx: 16 (over z_hi, y), smp: 8 (over x, core), dp: 2 (over z_lo).
Axes of the slice: x: 4, y: 4, z: 8 (z_hi: 4, z_lo: 2; z = z_hi * 2 + z_lo), core: 2. Of those that a mesh axis runs over, the one named last changes fastest.
Arguments:
- queries: bfloat16 [16, 2048, 4096], P(('dp', 'smp'), 'ctx'), parts along dimension 0, may hold values from -64 to 64
- key_prefix: bfloat16 [2048, 512], P(('dp', 'ctx')), parts along dimension 0, may hold values from -16 to 16
- value_prefix: bfloat16 [2048, 512], P(('dp', 'ctx')), parts along dimension 0, may hold values from -6 to 6
- key_response: bfloat16 [16, 2048, 512], P(('dp', 'smp'), 'ctx'), parts along dimension 0, may hold values from -6 to 6
- value_response: bfloat16 [16, 2048, 512], P(('dp', 'smp'), 'ctx'), parts along dimension 0, may hold values from -6 to 6
- output_gradient: bfloat16 [16, 2048, 4096], P(('dp', 'smp'), 'ctx'), parts along dimension 0, may hold values from -6 to 6
- lengths: int32 [32], P('dp'), parts along dimension 0, may hold values from 1 to 1024, as said below
- assign: int32 [32], P('dp'), parts along dimension 0, may hold values from 0 to 7, as said below
Outputs:
- grad_queries: bfloat16 [16, 2048, 4096], P(('dp', 'smp'), 'ctx'), parts along dimension 0
- grad_key_prefix: bfloat16 [2048, 512], P(('dp', 'ctx')), parts along dimension 0
- grad_value_prefix: bfloat16 [2048, 512], P(('dp', 'ctx')), parts along dimension 0
- grad_key_response: bfloat16 [16, 2048, 512], P(('dp', 'smp'), 'ctx'), parts along dimension 0
- grad_value_response: bfloat16 [16, 2048, 512], P(('dp', 'smp'), 'ctx'), parts along dimension 0
The draws below stay inside these ranges and needn't reach their ends.
There are 2 independent parts, one for each index of `dp`. The reference program is written for one: setup_inputs(seed, part) draws one part's arguments, and reference() takes and returns one part's arrays. A program takes and returns all parts, laid end to end along the dimension named above; each array names one. Nothing has to cross between parts.
Inputs may be any that keep to these rules, and one draw needn't show every extreme that they name: One response has exactly 1024 tokens; every other response has 256 to 512 tokens; the lengths on one index of smp sum to at most 2048. `assign`: every index of smp is named by one to three responses.
All inputs are finite; a program needn't handle non-finite values.
Results may differ from the reference program's by a relative error of at most 0.0057.
Values may be sent and summed in bfloat16 or wider, within the bound.
A program may use at most 128 MiB of HBM per device.

```python
import jax
import jax.numpy as jnp
from jax import lax

QUERY_HEADS = 32
KEY_HEADS = 4
HEAD_SIZE = 128
GROUP_QUERIES = 8
KVW = 512
RESPONSE_SLOTS = 2048
PREFIX_TOKENS = 1024
N_RESP = 16
N_SMP = 8


def prefix_base(key):
    return jnp.clip(jax.random.normal(jax.random.fold_in(key, 31), (PREFIX_TOKENS, KEY_HEADS * HEAD_SIZE), jnp.float32), -5.0, 5.0)


def response_plan(key):
    order = jax.random.permutation(jax.random.fold_in(key, 24), N_RESP)
    index_order = jax.random.permutation(jax.random.fold_in(key, 22), N_SMP).astype(jnp.int32)
    places = jnp.arange(N_RESP, dtype=jnp.int32)
    position = jnp.where(places == 0, 0, 1 + (places - 1) % (N_SMP - 1))
    coins = jax.random.randint(jax.random.fold_in(key, 23), (N_RESP,), 0, 2)
    movable = (places >= 1) & (places <= N_RESP - N_SMP) & (coins == 1)
    moved_count = jnp.cumsum(movable.astype(jnp.int32))
    pulled = movable & (moved_count <= 2)
    position = jnp.where(pulled, 0, position)
    owner = index_order[position].astype(jnp.int32)
    short_spans = jax.random.randint(jax.random.fold_in(key, 21), (N_RESP,), RESPONSE_SLOTS // 8, RESPONSE_SLOTS // 4 + 1)
    spans = jnp.where(places == 0, RESPONSE_SLOTS // 2, short_spans).astype(jnp.int32)
    assign = jnp.zeros((N_RESP,), jnp.int32).at[order].set(owner)
    lengths = jnp.zeros((N_RESP,), jnp.int32).at[order].set(spans)
    return (lengths, assign)


def draw_lengths(key, part):
    return response_plan(key)[0]


def draw_assign(key, part):
    return response_plan(key)[1]


def draw_key_prefix(key, part):
    base = prefix_base(key)
    return base.astype(jnp.bfloat16)


def draw_queries(key, part):
    key = jax.random.fold_in(key, 2)
    value_rows = jnp.clip(jax.random.normal(key, (N_SMP, RESPONSE_SLOTS, QUERY_HEADS * HEAD_SIZE), jnp.float32), -6.0, 6.0)
    return value_rows.astype(jnp.bfloat16)


def levels(own_key, dims, split, least, top_value):
    def one(dim, shards_of):
        heights = jax.random.uniform(jax.random.fold_in(jax.random.fold_in(own_key, 6), dim), (shards_of,), jnp.float32, least / len(split), top_value / len(split))
        return jnp.repeat(jnp.exp(heights), dims[dim] // shards_of).reshape((-1,) + (1,) * (len(dims) - dim - 1))

    level = one(*split[0])
    for cut in split[1:]:
        level = level * one(*cut)
    return level


def centred(rng, extent, scale, reach, pieces=(), kind=jnp.bfloat16):
    array = scale * jax.random.normal(rng, extent, jnp.float32)
    if pieces:
        array = array * levels(rng, extent, pieces, -0.22, 0.18)
    return jnp.clip(array, -reach, reach).astype(kind)


def setup_inputs(seed: int = 0, part: int = 0) -> dict:
    arg_keys = jax.random.split(jax.random.key(seed), 9)
    part_splits = jax.random.split(jax.random.fold_in(arg_keys[8], part), 9)
    return {
        "queries": draw_queries(jax.random.fold_in(jax.random.fold_in(arg_keys[8], part), 71), part),
        "key_prefix": draw_key_prefix(jax.random.fold_in(jax.random.fold_in(arg_keys[8], part), 71), part),
        "value_prefix": centred(part_splits[2], (PREFIX_TOKENS, KVW), 1.0, 6.0, ((0, 16),)),
        "key_response": centred(part_splits[3], (N_SMP, RESPONSE_SLOTS, KVW), 1.0, 6.0, ((0, 8), (1, 16))),
        "value_response": centred(part_splits[4], (N_SMP, RESPONSE_SLOTS, KVW), 1.0, 6.0, ((0, 8), (1, 16))),
        "output_gradient": centred(part_splits[5], (N_SMP, RESPONSE_SLOTS, QUERY_HEADS * HEAD_SIZE), 1.0, 6.0, ((0, 8), (1, 16))),
        "lengths": draw_lengths(jax.random.fold_in(jax.random.fold_in(arg_keys[8], part), 71), part),
        "assign": draw_assign(jax.random.fold_in(jax.random.fold_in(arg_keys[8], part), 71), part),
    }


NEG = -1.0e30


def rounded(value):
    return lax.optimization_barrier(value.astype(jnp.bfloat16)).astype(jnp.float32)


def segments_of(lengths, assign, sample_index):
    on_index = (assign == sample_index).astype(jnp.int32)
    spans = lengths * on_index
    ends = jnp.cumsum(spans).astype(jnp.int32)
    starts = ends - spans
    slots = jnp.arange(RESPONSE_SLOTS, dtype=jnp.int32)
    inside = (slots[:, None] >= starts[None, :]) & (slots[:, None] < ends[None, :]) & (on_index[None, :] > 0)
    number = jnp.arange(N_RESP, dtype=jnp.int32) + 1
    return (jnp.sum(inside.astype(jnp.int32) * number[None, :], axis=1) - 1).astype(jnp.int32)


def reference(queries, key_prefix, value_prefix, key_response, value_response, output_gradient, lengths, assign):
    scale = HEAD_SIZE ** -0.5
    slots = jnp.arange(RESPONSE_SLOTS, dtype=jnp.int32)
    prefix_key_gradient = jnp.zeros((PREFIX_TOKENS, KEY_HEADS * HEAD_SIZE), jnp.float32)
    prefix_value_gradient = jnp.zeros((PREFIX_TOKENS, KEY_HEADS * HEAD_SIZE), jnp.float32)
    out_q, out_k, out_v = [], [], []
    for sample_index in range(N_SMP):
        seg = segments_of(lengths, assign, sample_index)
        live = seg >= 0
        self_mask = (seg[:, None] == seg[None, :]) & (slots[None, :] <= slots[:, None]) & live[:, None]
        mask = jnp.concatenate([jnp.broadcast_to(live[:, None], (RESPONSE_SLOTS, PREFIX_TOKENS)), self_mask], axis=1)
        key_rows = jnp.concatenate([key_prefix, key_response[sample_index]], axis=0).astype(jnp.float32)
        value_rows = jnp.concatenate([value_prefix, value_response[sample_index]], axis=0).astype(jnp.float32)
        query_head_split = queries[sample_index].astype(jnp.float32).reshape(RESPONSE_SLOTS, KEY_HEADS, GROUP_QUERIES, HEAD_SIZE).transpose(1, 0, 2, 3)
        output_gradient_heads = output_gradient[sample_index].astype(jnp.float32).reshape(RESPONSE_SLOTS, KEY_HEADS, GROUP_QUERIES, HEAD_SIZE).transpose(1, 0, 2, 3)
        key_head_split = key_rows.reshape(-1, KEY_HEADS, HEAD_SIZE).transpose(1, 0, 2)
        value_head_split = value_rows.reshape(-1, KEY_HEADS, HEAD_SIZE).transpose(1, 0, 2)

        def per_head(operands):
            q_one, do_one, k_one, v_one = operands
            score = scale * jnp.einsum('tgd,nd->gtn', q_one, k_one)
            score = jnp.where(mask[None], score, NEG)
            top = jnp.max(score, axis=-1, keepdims=True)
            total = jnp.sum(jnp.where(mask[None], jnp.exp(score - top), 0.0), axis=-1, keepdims=True)
            total = jnp.where(live[None, :, None], total, 1.0)
            lse = jnp.where(live[None, :, None], top + jnp.log(total), 0.0)
            prob = jnp.where(mask[None], jnp.exp(score - lse), 0.0)
            dprob = jnp.einsum('tgd,nd->gtn', do_one, v_one)
            delta = jnp.sum(prob * dprob, axis=-1, keepdims=True)
            dscore = prob * (dprob - delta)
            prob_b = rounded(prob)
            dscore_b = rounded(dscore)
            dq_one = scale * jnp.einsum('gtn,nd->tgd', dscore_b, k_one)
            dk_one = scale * jnp.einsum('gtn,tgd->nd', dscore_b, q_one)
            dv_one = jnp.einsum('gtn,tgd->nd', prob_b, do_one)
            return dq_one, dk_one, dv_one

        dq_all, key_gradient_full, value_gradient_full = lax.map(per_head, (query_head_split, output_gradient_heads, key_head_split, value_head_split))
        dq_all = dq_all.transpose(1, 0, 2, 3).reshape(RESPONSE_SLOTS, QUERY_HEADS * HEAD_SIZE)
        key_gradient_full = key_gradient_full.transpose(1, 0, 2).reshape(-1, KEY_HEADS * HEAD_SIZE)
        value_gradient_full = value_gradient_full.transpose(1, 0, 2).reshape(-1, KEY_HEADS * HEAD_SIZE)
        prefix_key_gradient = prefix_key_gradient + key_gradient_full[:PREFIX_TOKENS]
        prefix_value_gradient = prefix_value_gradient + value_gradient_full[:PREFIX_TOKENS]
        out_q.append(dq_all.astype(jnp.bfloat16))
        out_k.append(key_gradient_full[PREFIX_TOKENS:].astype(jnp.bfloat16))
        out_v.append(value_gradient_full[PREFIX_TOKENS:].astype(jnp.bfloat16))
    return (jnp.stack(out_q), prefix_key_gradient.astype(jnp.bfloat16), prefix_value_gradient.astype(jnp.bfloat16), jnp.stack(out_k), jnp.stack(out_v))
```

```python
import functools

import jax
import jax.numpy as jnp
from jax import lax
from jax.experimental import pallas as pl
from jax.experimental.pallas import tpu as pltpu
from jax.sharding import PartitionSpec as P

HEADS = 4
GROUP = 8
DIM = 128
ROWS = 128
PREFIX = 1024
WINDOW = 9 * ROWS
KEYS = PREFIX + WINDOW
QB = 256
STEPS = GROUP * ROWS // QB
SIDE = 4
SCALE = DIM ** -0.5
LOG2E = 1.4426950408889634
MASKED = -1e30
RESPONSES = 16
MESH = pl.DeviceIdType.MESH


def dot_nt(a, b):
    return lax.dot_general(a, b, (((1,), (1,)), ((), ())), preferred_element_type=jnp.float32)


def dot_nn(a, b):
    return lax.dot_general(a, b, (((1,), (0,)), ((), ())), preferred_element_type=jnp.float32)


def fold(x, op):
    return op(x.reshape(x.shape[0] // 8, 8, x.shape[1]), axis=0)


def attend(h, qb, q_v, do_v, pre, win, bias, live, s_scr, dp_scr, acc, kt, dq_v):
    col = pl.multiple_of(h * (GROUP * DIM) + qb * QB, QB)
    qa = q_v[:, pl.ds(col, QB)]
    da = do_v[:, pl.ds(col, QB)]
    qs = jnp.concatenate([qa[:, :DIM], qa[:, DIM:]], axis=0)
    ds_ = jnp.concatenate([da[:, :DIM], da[:, DIM:]], axis=0)
    chunks = [(256 * i, 256) for i in range(4)] + [(PREFIX + 384 * i, 384) for i in range(3)]

    def rows_of(kv, start, size):
        if start < PREFIX:
            return pre[h, kv, pl.ds(start, size), :]
        return win[h, kv, pl.ds((start - PREFIX) // ROWS, size // ROWS)].reshape(size, DIM)

    top8 = jnp.full((8, QB), MASKED, jnp.float32)
    for start, size in chunks:
        s = dot_nt(rows_of(0, start, size), qs)
        if start >= PREFIX:
            b = bias[pl.ds(start - PREFIX, size), :]
            s = s + jnp.concatenate([b, b], axis=1)
        s_scr[pl.ds(start, size), :] = s
        top8 = jnp.maximum(top8, fold(s, jnp.max))
    factor = SCALE * LOG2E
    shift = jnp.max(top8, axis=0, keepdims=True) * factor
    sum8 = jnp.zeros((8, QB), jnp.float32)
    dot8 = jnp.zeros((8, QB), jnp.float32)
    for start, size in chunks:
        p = jnp.exp2(s_scr[pl.ds(start, size), :] * factor - shift)
        dp = dot_nt(rows_of(1, start, size), ds_)
        s_scr[pl.ds(start, size), :] = p
        dp_scr[pl.ds(start, size), :] = dp
        sum8 = sum8 + fold(p, jnp.sum)
        dot8 = dot8 + fold(p * dp, jnp.sum)
    inverse = 1.0 / jnp.sum(sum8, axis=0, keepdims=True)
    delta = jnp.sum(dot8, axis=0, keepdims=True) * inverse
    live_row = live[...]
    inverse = inverse * jnp.concatenate([live_row, live_row], axis=1)
    dqt = jnp.zeros((DIM, QB), jnp.float32)
    for start, size in chunks:
        p = s_scr[pl.ds(start, size), :] * inverse
        dsc = (p * (dp_scr[pl.ds(start, size), :] - delta)).astype(jnp.bfloat16)
        pb = p.astype(jnp.bfloat16)
        acc[h, 1, pl.ds(start, size), :] += dot_nn(pb, ds_)
        acc[h, 0, pl.ds(start, size), :] += dot_nn(dsc, qs)
        dqt = dqt + dot_nn(kt[:, pl.ds(start, size)], dsc)
    dq = (dqt * SCALE).T.astype(jnp.bfloat16)
    dq_v[:, pl.ds(col, QB)] = jnp.concatenate([dq[:ROWS], dq[ROWS:]], axis=1)


def transpose_keys(h, pre, win, kt):
    for i in range(4):
        kt[:, pl.ds(256 * i, 256)] = pre[h, 0, pl.ds(256 * i, 256), :].T
    for i in range(9):
        kt[:, pl.ds(PREFIX + ROWS * i, ROWS)] = win[h, 0, i].T


def masks(place, smp, len_ref, asg_ref, bias, live):
    slot = place * ROWS + lax.broadcasted_iota(jnp.int32, (1, ROWS), 1)
    first = jnp.full((1, ROWS), 1 << 20, jnp.int32)
    start = jnp.int32(0)
    for r in range(RESPONSES):
        stop = start + jnp.where(asg_ref[r] == smp, len_ref[r], 0)
        first = jnp.where((slot >= start) & (slot < stop), start, first)
        start = stop
    live[...] = jnp.where(first < (1 << 20), 1.0, 0.0).astype(jnp.float32)
    for i in range(9):
        key = (place - 8 + i) * ROWS + lax.broadcasted_iota(jnp.int32, (ROWS, ROWS), 0)
        allowed = (key >= first) & (key <= slot)
        bias[pl.ds(i * ROWS, ROWS), :] = jnp.where(allowed, 0.0, MASKED).astype(jnp.float32)


def kernel(
    q_hbm, kp_hbm, vp_hbm, kr_hbm, vr_hbm, do_hbm, len_ref, asg_ref,
    dq_hbm, dkp_hbm, dvp_hbm, dkr_hbm, dvr_hbm,
    q_v, do_v, dq_v, pre, win, bias, live, s_scr, dp_scr, acc, kt,
    rsend, rrecv, zsend, zrecv,
    csend, crecv, xsend, xrecv, ysend, yrecv, wsend, wrecv, finall,
    okr, okp,
    local, gz_s, gz_r, gy_s, gy_r, pz_s, pz_r, py_s, py_r, px_s, px_r, pc_s, pc_r,
    ry_s, ry_r, rz_s, rz_r, rc_s, rc_r, rx_s, rx_r, rp_s, rp_r, rw_s, rw_r, rf_s, rf_r,
):
    ctx = lax.axis_index("ctx")
    smp = lax.axis_index("smp")
    z, y = ctx // SIDE, ctx % SIDE
    x, core = smp // 2, smp % 2
    other = 1 - core

    def at_z(o):
        return {"ctx": ((z + o) % SIDE) * SIDE + y}

    def at_y(o):
        return {"ctx": z * SIDE + (y + o) % SIDE}

    def at_x(o):
        return {"smp": ((x + o) % SIDE) * 2 + core}

    at_core = {"smp": x * 2 + other}

    def send(src, dst, ss, rs, where):
        return pltpu.make_async_remote_copy(
            src_ref=src, dst_ref=dst, send_sem=ss, recv_sem=rs, device_id=where, device_id_type=MESH
        )

    loads = []
    for h in range(HEADS):
        cols = pl.ds(h * DIM, DIM)
        loads.append(pltpu.make_async_copy(kr_hbm.at[0, :, cols], win.at[h, 0, 8], local.at[2 * h]))
        loads.append(pltpu.make_async_copy(vr_hbm.at[0, :, cols], win.at[h, 1, 8], local.at[2 * h + 1]))
    mine = pl.ds(pl.multiple_of(x * 256 + y * 64 + z * 16, 16), 16)
    from_rows = pl.ds(pl.multiple_of(x * 16, 16), 16)

    def load_prefix(h, src):
        return pltpu.make_async_copy(
            src.at[from_rows, pl.ds(h * DIM, DIM)], pre.at[h, core, mine, :], local.at[8 + h]
        )

    for copy in loads:
        copy.start()

    @pl.when(core == 0)
    def _():
        for h in range(HEADS):
            load_prefix(h, kp_hbm).start()

    @pl.when(core == 1)
    def _():
        for h in range(HEADS):
            load_prefix(h, vp_hbm).start()

    load_q = pltpu.make_async_copy(q_hbm.at[0], q_v, local.at[12])
    load_do = pltpu.make_async_copy(do_hbm.at[0], do_v, local.at[13])
    load_q.start()
    load_do.start()

    barrier = pltpu.get_barrier_semaphore()
    partners = [at_z(o) for o in (1, 2, 3)] + [at_y(o) for o in (1, 2, 3)]
    smp_partners = [{"smp": (smp + o) % 8} for o in range(1, 8)]
    for where in partners + smp_partners:
        pl.semaphore_signal(barrier, inc=1, device_id=where, device_id_type=MESH)
    for copy in loads:
        copy.wait()
    for h in range(HEADS):
        load_prefix(h, kp_hbm).wait()
    pl.semaphore_wait(barrier, len(partners) + len(smp_partners))

    def gather_z(h, step):
        src, dst = (8, 4) if step == 0 else (4, 0)
        return send(win.at[h, :, src], win.at[h, :, dst], gz_s.at[h, step], gz_r.at[h, step], at_z(1))

    def gather_y(h, o, part):
        d = jnp.where(y + o < SIDE, o, o - SIDE)
        if part == 0:
            src, dst = 4, 4 - d
        else:
            src, dst = jnp.where(d > 0, 8, 0), jnp.where(d > 0, 8 - d, -d)
        return send(win.at[h, :, src], win.at[h, :, dst], gy_s.at[h, o - 1, part], gy_r.at[h, o - 1, part], at_y(o))

    def gather_a(h):
        gather_z(h, 0).start()

    def gather_b(h):
        gather_z(h, 0).wait_recv()
        gather_z(h, 1).start()
        for o in (1, 2, 3):
            gather_y(h, o, 0).start()

    def gather_c(h):
        gather_z(h, 1).wait_recv()
        for o in (1, 2, 3):
            gather_y(h, o, 1).start()

    def gather_d(h):
        for o in (1, 2, 3):
            gather_y(h, o, 0).wait_recv()
            gather_y(h, o, 1).wait_recv()

    def prefix_z(o):
        return send(pre.at[:, core, mine, :], pre.at[:, core, mine, :], pz_s.at[o - 1], pz_r.at[o - 1], at_z(o))

    def prefix_y(o):
        rows = pl.ds(pl.multiple_of(x * 256 + y * 64, 64), 64)
        return send(pre.at[:, core, rows, :], pre.at[:, core, rows, :], py_s.at[o - 1], py_r.at[o - 1], at_y(o))

    def prefix_x(h, o):
        rows = pl.ds(pl.multiple_of(x * 256, 256), 256)
        return send(
            pre.at[h, core, rows, :], pre.at[h, core, rows, :], px_s.at[h, o - 1], px_r.at[h, o - 1], at_x(o)
        )

    def prefix_c(h):
        return send(pre.at[h, core], pre.at[h, core], pc_s.at[h], pc_r.at[h], at_core)

    def prefix_last(h):
        for o in (1, 2, 3):
            prefix_x(h, o).wait_recv()
        prefix_c(h).start()

    def reduce_y(h, o, part):
        d = jnp.where(y + o < SIDE, o, o - SIDE)
        src = 4 + d if part == 0 else jnp.where(d > 0, d, 8 + d)
        return send(
            rsend.at[h, src], rrecv.at[h, o - 1, part], ry_s.at[h, o - 1, part], ry_r.at[h, o - 1, part], at_y(o)
        )

    def reduce_z(h, step):
        return send(zsend.at[h, step], zrecv.at[h, step], rz_s.at[h, step], rz_r.at[h, step], at_z(3))

    def slot_rows(i):
        return pl.ds(PREFIX + i * ROWS, ROWS)

    def reduce_a(h):
        for i in range(9):
            for kv in range(2):
                rsend[h, i, kv] = acc[h, kv, slot_rows(i), :].astype(jnp.bfloat16)
        for o in (1, 2, 3):
            for part in (1, 0):
                reduce_y(h, o, part).start()

    def reduce_b(h):
        for o in (1, 2, 3):
            reduce_y(h, o, 0).wait_recv()
            reduce_y(h, o, 1).wait_recv()
        for kv in range(2):
            far = acc[h, kv, slot_rows(0), :]
            mid = acc[h, kv, slot_rows(4), :]
            near = acc[h, kv, slot_rows(8), :]
            for o in (1, 2, 3):
                mid = mid + rrecv[h, o - 1, 0, kv].astype(jnp.float32)
                term = rrecv[h, o - 1, 1, kv].astype(jnp.float32)
                lower = jnp.where(y >= o, 1.0, 0.0).astype(jnp.float32)
                far = far + term * lower
                near = near + term * (1.0 - lower)
            zsend[h, 0, kv] = far.astype(jnp.bfloat16)
            acc[h, kv, slot_rows(4), :] = mid
            acc[h, kv, slot_rows(8), :] = near
        reduce_z(h, 0).start()

    def reduce_c(h):
        reduce_z(h, 0).wait_recv()
        for kv in range(2):
            mid = acc[h, kv, slot_rows(4), :] + zrecv[h, 0, kv].astype(jnp.float32)
            zsend[h, 1, kv] = mid.astype(jnp.bfloat16)
        reduce_z(h, 1).start()

    def reduce_d(h):
        reduce_z(h, 1).wait_recv()
        for kv in range(2):
            near = acc[h, kv, slot_rows(8), :] + zrecv[h, 1, kv].astype(jnp.float32)
            if kv == 0:
                near = near * SCALE
            okr[kv, h] = near.astype(jnp.bfloat16)

    def total_c(h):
        return send(csend.at[h], crecv.at[h], rc_s.at[h], rc_r.at[h], at_core)

    def total_x(h, o):
        return send(
            xsend.at[h, (x + o) % SIDE], xrecv.at[h, o - 1], rx_s.at[h, o - 1], rx_r.at[h, o - 1], at_x(o)
        )

    def total_y(h, o):
        return send(
            ysend.at[h, (y + o) % SIDE], yrecv.at[h, o - 1], rp_s.at[h, o - 1], rp_r.at[h, o - 1], at_y(o)
        )

    def total_z(h, o):
        return send(
            wsend.at[h, (z + o) % SIDE], wrecv.at[h, o - 1], rw_s.at[h, o - 1], rw_r.at[h, o - 1], at_z(o)
        )

    def total_a(h):
        csend[h] = acc[h, other, pl.ds(0, PREFIX), :].astype(jnp.bfloat16)
        total_c(h).start()

    def total_b(h):
        total_c(h).wait_recv()
        for i in range(SIDE):
            rows = pl.ds(256 * i, 256)
            both = acc[h, core, rows, :] + crecv[h, rows, :].astype(jnp.float32)
            acc[h, core, rows, :] = both
            xsend[h, i] = both.astype(jnp.bfloat16)
        for o in (1, 2, 3):
            total_x(h, o).start()

    def total_d(h):
        for o in (1, 2, 3):
            total_x(h, o).wait_recv()
        whole = acc[h, core, pl.ds(pl.multiple_of(x * 256, 256), 256), :]
        for o in (1, 2, 3):
            whole = whole + xrecv[h, o - 1].astype(jnp.float32)
        ysend[h] = whole.reshape(SIDE, 64, DIM)
        for o in (1, 2, 3):
            total_y(h, o).start()

    def total_e(h):
        for o in (1, 2, 3):
            total_y(h, o).wait_recv()
        whole = ysend[h, y]
        for o in (1, 2, 3):
            whole = whole + yrecv[h, o - 1]
        wsend[h] = whole.reshape(SIDE, 16, DIM)
        for o in (1, 2, 3):
            total_z(h, o).start()

    def total_f(h):
        for o in (1, 2, 3):
            total_z(h, o).wait_recv()
        whole = wsend[h, z]
        for o in (1, 2, 3):
            whole = whole + wrecv[h, o - 1]
        whole = whole * jnp.where(core == 0, SCALE, 1.0).astype(jnp.float32)
        finall[smp, h] = whole.astype(jnp.bfloat16)

    def total_g(o):
        return send(finall.at[smp], finall.at[smp], rf_s.at[o - 1], rf_r.at[o - 1], smp_partners[o - 1])

    for o in (1, 2, 3):
        prefix_z(o).start()
    gather_a(0)
    masks(ctx, smp, len_ref, asg_ref, bias, live)
    for o in (1, 2, 3):
        prefix_z(o).wait_recv()
    for o in (1, 2, 3):
        prefix_y(o).start()
    gather_b(0)
    gather_a(1)
    acc[...] = jnp.zeros_like(acc)
    for o in (1, 2, 3):
        prefix_y(o).wait_recv()
    for h in range(HEADS):
        for o in (1, 2, 3):
            prefix_x(h, o).start()
    load_q.wait()
    load_do.wait()
    gather_c(0)
    prefix_last(0)
    gather_b(1)
    gather_a(2)
    gather_d(0)
    prefix_c(0).wait_recv()

    @pl.loop(0, HEADS * STEPS)
    def _(it):
        h, qb = it // STEPS, it % STEPS

        @pl.when((qb == 0) & (h > 0))
        def _():
            gather_d(h)
            prefix_c(h).wait_recv()

        @pl.when(qb == 0)
        def _():
            transpose_keys(h, pre, win, kt)

        attend(h, qb, q_v, do_v, pre, win, bias, live, s_scr, dp_scr, acc, kt, dq_v)

        @pl.when((qb == 0) & (h > 0))
        def _():
            total_b(h - 1)
            reduce_b(h - 1)

        @pl.when((qb == 0) & (h + 1 < HEADS))
        def _():
            gather_c(h + 1)
            prefix_last(h + 1)

        @pl.when((qb == 1) & (h + 2 < HEADS))
        def _():
            gather_b(h + 2)

        @pl.when((qb == 1) & (h + 3 < HEADS))
        def _():
            gather_a(h + 3)

        @pl.when((qb == 1) & (h > 0))
        def _():
            total_d(h - 1)
            reduce_c(h - 1)

        @pl.when((qb == 2) & (h > 0))
        def _():
            total_e(h - 1)
            reduce_d(h - 1)

        @pl.when((qb == 3) & (h > 0))
        def _():
            total_f(h - 1)

        @pl.when(qb == STEPS - 1)
        def _():
            total_a(h)
            reduce_a(h)

    store_q = pltpu.make_async_copy(dq_v, dq_hbm.at[0], local.at[12])
    store_q.start()
    last = HEADS - 1
    total_b(last)
    reduce_b(last)
    total_d(last)
    reduce_c(last)
    total_e(last)
    total_f(last)
    for o in range(1, 8):
        total_g(o).start()
    reduce_d(last)
    stores = []
    for h in range(HEADS):
        cols = pl.ds(h * DIM, DIM)
        stores.append(pltpu.make_async_copy(okr.at[0, h], dkr_hbm.at[0, :, cols], local.at[2 * h]))
        stores.append(pltpu.make_async_copy(okr.at[1, h], dvr_hbm.at[0, :, cols], local.at[2 * h + 1]))
    for copy in stores:
        copy.start()
    for o in range(1, 8):
        total_g(o).wait_recv()
    for kv in range(2):
        for a in range(SIDE):
            for h in range(HEADS):
                okp[kv, pl.ds(16 * a, 16), pl.ds(h * DIM, DIM)] = finall[2 * a + kv, h]
    tail = [
        pltpu.make_async_copy(okp.at[0], dkp_hbm, local.at[8]),
        pltpu.make_async_copy(okp.at[1], dvp_hbm, local.at[9]),
    ]
    for copy in tail:
        copy.start()

    for o in (1, 2, 3):
        prefix_z(o).wait_send()
        prefix_y(o).wait_send()
    for o in range(1, 8):
        total_g(o).wait_send()

    @pl.loop(0, HEADS)
    def _(h):
        prefix_c(h).wait_send()
        total_c(h).wait_send()
        for step in range(2):
            gather_z(h, step).wait_send()
            reduce_z(h, step).wait_send()
        for o in (1, 2, 3):
            prefix_x(h, o).wait_send()
            total_x(h, o).wait_send()
            total_y(h, o).wait_send()
            total_z(h, o).wait_send()
            for part in range(2):
                gather_y(h, o, part).wait_send()
                reduce_y(h, o, part).wait_send()

    for copy in stores + tail + [store_q]:
        copy.wait()


def shards(q, kp, vp, kr, vr, do, lengths, assign):
    bf, f32 = jnp.bfloat16, jnp.float32
    dma = pltpu.SemaphoreType.DMA
    hbm = pl.BlockSpec(memory_space=pl.ANY)
    smem = pl.BlockSpec(memory_space=pltpu.SMEM)
    H = HEADS
    return pl.pallas_call(
        kernel,
        out_shape=(
            jax.ShapeDtypeStruct(q.shape, bf),
            jax.ShapeDtypeStruct(kp.shape, bf),
            jax.ShapeDtypeStruct(vp.shape, bf),
            jax.ShapeDtypeStruct(kr.shape, bf),
            jax.ShapeDtypeStruct(vr.shape, bf),
        ),
        in_specs=[hbm] * 6 + [smem] * 2,
        out_specs=(hbm,) * 5,
        scratch_shapes=[
            pltpu.VMEM((ROWS, H * GROUP * DIM), bf),
            pltpu.VMEM((ROWS, H * GROUP * DIM), bf),
            pltpu.VMEM((ROWS, H * GROUP * DIM), bf),
            pltpu.VMEM((H, 2, PREFIX, DIM), bf),
            pltpu.VMEM((H, 2, 9, ROWS, DIM), bf),
            pltpu.VMEM((WINDOW, ROWS), f32),
            pltpu.VMEM((1, ROWS), f32),
            pltpu.VMEM((KEYS, QB), f32),
            pltpu.VMEM((KEYS, QB), f32),
            pltpu.VMEM((H, 2, KEYS, DIM), f32),
            pltpu.VMEM((DIM, KEYS), bf),
            pltpu.VMEM((H, 9, 2, ROWS, DIM), bf),
            pltpu.VMEM((H, 3, 2, 2, ROWS, DIM), bf),
            pltpu.VMEM((H, 2, 2, ROWS, DIM), bf),
            pltpu.VMEM((H, 2, 2, ROWS, DIM), bf),
            pltpu.VMEM((H, PREFIX, DIM), bf),
            pltpu.VMEM((H, PREFIX, DIM), bf),
            pltpu.VMEM((H, SIDE, 256, DIM), bf),
            pltpu.VMEM((H, 3, 256, DIM), bf),
            pltpu.VMEM((H, SIDE, 64, DIM), f32),
            pltpu.VMEM((H, 3, 64, DIM), f32),
            pltpu.VMEM((H, SIDE, 16, DIM), f32),
            pltpu.VMEM((H, 3, 16, DIM), f32),
            pltpu.VMEM((8, H, 16, DIM), bf),
            pltpu.VMEM((2, H, ROWS, DIM), bf),
            pltpu.VMEM((2, 64, H * DIM), bf),
            dma((14,)),
            dma((H, 2)), dma((H, 2)), dma((H, 3, 2)), dma((H, 3, 2)),
            dma((3,)), dma((3,)), dma((3,)), dma((3,)),
            dma((H, 3)), dma((H, 3)), dma((H,)), dma((H,)),
            dma((H, 3, 2)), dma((H, 3, 2)), dma((H, 2)), dma((H, 2)),
            dma((H,)), dma((H,)), dma((H, 3)), dma((H, 3)),
            dma((H, 3)), dma((H, 3)), dma((H, 3)), dma((H, 3)),
            dma((7,)), dma((7,)),
        ],
        compiler_params=pltpu.CompilerParams(
            collective_id=0, has_side_effects=True, vmem_limit_bytes=56 * 1024 * 1024
        ),
        name="attention_backward",
    )(q, kp, vp, kr, vr, do, lengths, assign)


def solution(mesh):
    rows = P(("dp", "smp"), "ctx", None)
    prefix = P(("dp", "ctx"), None)
    return jax.shard_map(
        shards,
        mesh=mesh,
        in_specs=(rows, prefix, prefix, rows, rows, rows, P("dp"), P("dp")),
        out_specs=(rows, prefix, prefix, rows, rows),
        check_vma=False,
    )
```

```python
import functools

import jax
import jax.numpy as jnp
from jax import lax
from jax.experimental import pallas as pl
from jax.experimental.pallas import tpu as pltpu
from jax.sharding import PartitionSpec as P

HEADS = 4
GROUP = 8
DIM = 128
ROWS = 128
PREFIX = 1024
WINDOW = 9 * ROWS
KEYS = PREFIX + WINDOW
QB = 512
KEPT = PREFIX + 3 * ROWS
SIDE = 4
SCALE = DIM ** -0.5
LOG2E = 1.4426950408889634
MASKED = -1e30
RESPONSES = 16
MESH = pl.DeviceIdType.MESH


def dot_nt(a, b):
    return lax.dot_general(a, b, (((1,), (1,)), ((), ())), preferred_element_type=jnp.float32)


def dot_nn(a, b):
    return lax.dot_general(a, b, (((1,), (0,)), ((), ())), preferred_element_type=jnp.float32)


def fold(x, op):
    return op(x.reshape(x.shape[0] // 8, 8, x.shape[1]), axis=0)


def head_rows(kv, h, start, size, pre, win):
    if start < PREFIX:
        return pre[h, kv, pl.ds(start, size), :]
    return win[h, kv, pl.ds((start - PREFIX) // ROWS, size // ROWS)].reshape(size, DIM)


def stacked(ref, h):
    parts = [ref[:, pl.ds(pl.multiple_of(h * (GROUP * DIM) + i * DIM, DIM), DIM)] for i in range(GROUP)]
    return jnp.concatenate(parts, axis=0)


def scores(h, half, qt, dot, pre, win, bias, live, s_scr, dp_scr, pb, dsb, slot):
    cols = pl.ds(half * QB, QB)
    qs = qt[h, :, cols]
    gs = dot[h, :, cols]
    chunks = [(i, ROWS) for i in range(0, KEYS, ROWS)]
    factor = SCALE * LOG2E
    stats = []
    for start, size in chunks:
        s = dot_nn(head_rows(0, h, start, size, pre, win), qs)
        dp = dot_nn(head_rows(1, h, start, size, pre, win), gs)
        if start >= PREFIX:
            b = bias[pl.ds(start - PREFIX, size), :]
            s = s + jnp.concatenate([b] * (QB // ROWS), axis=1)
        top = fold(s, jnp.max) * factor
        p = jnp.exp2((s * factor).reshape(size // 8, 8, QB) - top[None]).reshape(size, QB)
        s_scr[pl.ds(start, size), :] = p
        dp_scr[pl.ds(start, size), :] = dp
        stats.append((top, fold(p, jnp.sum), fold(p * dp, jnp.sum)))
    whole = functools.reduce(jnp.maximum, [t for t, _, _ in stats])
    whole = jnp.max(whole, axis=0, keepdims=True)
    factors = [jnp.exp2(t - whole) for t, _, _ in stats]
    total = sum(t[1] * f for t, f in zip(stats, factors))
    dotted = sum(t[2] * f for t, f in zip(stats, factors))
    inverse = 1.0 / jnp.sum(total, axis=0, keepdims=True)
    delta = jnp.sum(dotted, axis=0, keepdims=True) * inverse
    live_row = live[...]
    inverse = inverse * jnp.concatenate([live_row] * (QB // ROWS), axis=1)
    for (start, size), f in zip(chunks, factors):
        rows = pl.ds(start, size)
        p = (s_scr[rows, :].reshape(size // 8, 8, QB) * (f * inverse)[None]).reshape(size, QB)
        pb[rows, cols] = p.astype(jnp.bfloat16)
        dsb[slot, rows, cols] = (p * (dp_scr[rows, :] - delta)).astype(jnp.bfloat16)


def prefix_terms(h, q_v, do_v, pb, dsb, acc, slot):
    rows = pl.ds(0, PREFIX)
    acc[h, 1, rows, :] = dot_nn(pb[rows, :], stacked(do_v, h))
    acc[h, 0, rows, :] = dot_nn(dsb[slot, rows, :], stacked(q_v, h))


def window_terms(h, q_v, do_v, pb, dsb, acc, rsend, slot):
    rows = pl.ds(PREFIX, WINDOW)
    for kv, term in ((1, dot_nn(pb[rows, :], stacked(do_v, h))), (0, dot_nn(dsb[slot, rows, :], stacked(q_v, h)))):
        for i in range(9):
            block = term[i * ROWS : (i + 1) * ROWS]
            rsend[h, i, kv] = block.astype(jnp.bfloat16)
            if i % 4 == 0:
                acc[h, kv, pl.ds(PREFIX + (i // 4) * ROWS, ROWS), :] = block


def query_terms(h, kt, dsb, dq_v, slot):
    dq = (dot_nn(kt[slot], dsb[slot]) * SCALE).T.astype(jnp.bfloat16)
    for i in range(GROUP):
        dq_v[:, pl.ds(pl.multiple_of(h * (GROUP * DIM) + i * DIM, DIM), DIM)] = dq[i * ROWS : (i + 1) * ROWS]


def transpose_keys(h, pre, win, kt, slot):
    for i in range(4):
        kt[slot, :, pl.ds(256 * i, 256)] = pre[h, 0, pl.ds(256 * i, 256), :].T
    for i in range(9):
        kt[slot, :, pl.ds(PREFIX + ROWS * i, ROWS)] = win[h, 0, i].T


def transpose_queries(ref, out):
    for h in range(HEADS):
        for i in range(GROUP):
            out[h, :, pl.ds(i * DIM, DIM)] = ref[:, pl.ds(h * (GROUP * DIM) + i * DIM, DIM)].T


def masks(place, smp, len_ref, asg_ref, bias, live):
    slot = place * ROWS + lax.broadcasted_iota(jnp.int32, (1, ROWS), 1)
    first = jnp.full((1, ROWS), 1 << 20, jnp.int32)
    start = jnp.int32(0)
    for r in range(RESPONSES):
        stop = start + jnp.where(asg_ref[r] == smp, len_ref[r], 0)
        first = jnp.where((slot >= start) & (slot < stop), start, first)
        start = stop
    live[...] = jnp.where(first < (1 << 20), 1.0, 0.0).astype(jnp.float32)
    for i in range(9):
        key = (place - 8 + i) * ROWS + lax.broadcasted_iota(jnp.int32, (ROWS, ROWS), 0)
        allowed = (key >= first) & (key <= slot)
        bias[pl.ds(i * ROWS, ROWS), :] = jnp.where(allowed, 0.0, MASKED).astype(jnp.float32)


def kernel(
    q_hbm, kp_hbm, vp_hbm, kr_hbm, vr_hbm, do_hbm, len_ref, asg_ref,
    dq_hbm, dkp_hbm, dvp_hbm, dkr_hbm, dvr_hbm,
    q_v, do_v, dq_v, qt, dot, pre, win, bias, live, s_scr, dp_scr, pb, dsb, acc, kt,
    rsend, rrecv, zsend, zrecv,
    csend, crecv, xsend, xrecv, ysend, ykept, yrecv, wsend, wrecv, finall,
    okr, okp,
    local, gz_s, gz_r, gy_s, gy_r, pz_s, pz_r, py_s, py_r, px_s, px_r, pc_s, pc_r,
    ry_s, ry_r, rz_s, rz_r, rc_s, rc_r, rx_s, rx_r, rp_s, rp_r, rw_s, rw_r, rf_s, rf_r,
):
    ctx = lax.axis_index("ctx")
    smp = lax.axis_index("smp")
    z, y = ctx // SIDE, ctx % SIDE
    x, core = smp // 2, smp % 2
    other = 1 - core

    three = (1, 2, 3)

    def at_z(o):
        return {"ctx": ((z + o) % SIDE) * SIDE + y}

    def at_y(o):
        return {"ctx": z * SIDE + (y + o) % SIDE}

    def at_x(o):
        return {"smp": ((x + o) % SIDE) * 2 + core}

    at_core = {"smp": x * 2 + other}

    def send(src, dst, ss, rs, where):
        return pltpu.make_async_remote_copy(
            src_ref=src, dst_ref=dst, send_sem=ss, recv_sem=rs, device_id=where, device_id_type=MESH
        )

    barrier = pltpu.get_barrier_semaphore()
    partners = [at_z(o) for o in (1, 2, 3)] + [at_y(o) for o in (1, 2, 3)]
    smp_partners = [{"smp": (smp + o) % 8} for o in range(1, 8)]
    for where in partners + smp_partners:
        pl.semaphore_signal(barrier, inc=1, device_id=where, device_id_type=MESH)
    loads = []
    for h in range(HEADS):
        cols = pl.ds(h * DIM, DIM)
        loads.append(pltpu.make_async_copy(kr_hbm.at[0, :, cols], win.at[h, 0, 8], local.at[2 * h]))
        loads.append(pltpu.make_async_copy(vr_hbm.at[0, :, cols], win.at[h, 1, 8], local.at[2 * h + 1]))
    mine = pl.ds(pl.multiple_of(x * 256 + y * 64 + z * 16, 16), 16)
    from_rows = pl.ds(pl.multiple_of(x * 16, 16), 16)

    def load_prefix(h, src):
        return pltpu.make_async_copy(
            src.at[from_rows, pl.ds(h * DIM, DIM)], pre.at[h, core, mine, :], local.at[8 + h]
        )

    for copy in loads:
        copy.start()

    @pl.when(core == 0)
    def _():
        for h in range(HEADS):
            load_prefix(h, kp_hbm).start()

    @pl.when(core == 1)
    def _():
        for h in range(HEADS):
            load_prefix(h, vp_hbm).start()

    load_q = pltpu.make_async_copy(q_hbm.at[0], q_v, local.at[12])
    load_do = pltpu.make_async_copy(do_hbm.at[0], do_v, local.at[13])
    load_q.start()
    load_do.start()

    masks(ctx, smp, len_ref, asg_ref, bias, live)
    for copy in loads:
        copy.wait()
    for h in range(HEADS):
        load_prefix(h, kp_hbm).wait()
    pl.semaphore_wait(barrier, len(partners) + len(smp_partners))

    def gather_z(h, step):
        dst = 4 - 4 * step
        return send(win.at[h, :, 8], win.at[h, :, dst], gz_s.at[h, step], gz_r.at[h, step], at_z(1 + step))

    def gather_y(h, o, part):
        d = jnp.where(y + o < SIDE, o, o - SIDE)
        if part == 0:
            src, dst = 4, 4 - d
        else:
            src, dst = jnp.where(d > 0, 8, 0), jnp.where(d > 0, 8 - d, -d)
        return send(win.at[h, :, src], win.at[h, :, dst], gy_s.at[h, o - 1, part], gy_r.at[h, o - 1, part], at_y(o))

    def gather_a(h):
        gather_z(h, 0).start()
        gather_z(h, 1).start()

    def gather_own(h):
        for o in three:
            @pl.when(y + o < SIDE)
            def _():
                gather_y(h, o, 1).start()

    def gather_b(h):
        gather_z(h, 0).wait_recv()
        for o in three:
            gather_y(h, o, 0).start()
        gather_z(h, 1).wait_recv()
        for o in three:
            @pl.when(y + o >= SIDE)
            def _():
                gather_y(h, o, 1).start()

    def gather_d(h):
        for o in (1, 2, 3):
            gather_y(h, o, 0).wait_recv()
            gather_y(h, o, 1).wait_recv()

    def some(h):
        return pl.ds(0, 1) if h == 0 else pl.ds(1, HEADS - 1)

    def prefix_z(h, o):
        part = pre.at[some(h), core, mine, :]
        return send(part, part, pz_s.at[h, o - 1], pz_r.at[h, o - 1], at_z(o))

    def prefix_y(h, o):
        rows = pl.ds(pl.multiple_of(x * 256 + y * 64, 64), 64)
        part = pre.at[some(h), core, rows, :]
        return send(part, part, py_s.at[h, o - 1], py_r.at[h, o - 1], at_y(o))

    def prefix_x(h, o):
        rows = pl.ds(pl.multiple_of(x * 256, 256), 256)
        return send(
            pre.at[h, core, rows, :], pre.at[h, core, rows, :], px_s.at[h, o - 1], px_r.at[h, o - 1], at_x(o)
        )

    def prefix_c(h):
        return send(pre.at[h, core], pre.at[h, core], pc_s.at[h], pc_r.at[h], at_core)

    def prefix_last(h):
        for o in (1, 2, 3):
            prefix_x(h, o).wait_recv()
        prefix_c(h).start()

    def reduce_y(h, o, part):
        d = jnp.where(y + o < SIDE, o, o - SIDE)
        src = 4 + d if part == 0 else jnp.where(d > 0, d, 8 + d)
        return send(
            rsend.at[h, src], rrecv.at[h, o - 1, part], ry_s.at[h, o - 1, part], ry_r.at[h, o - 1, part], at_y(o)
        )

    def reduce_z(h, step):
        return send(zsend.at[h, step], zrecv.at[h, step], rz_s.at[h, step], rz_r.at[h, step], at_z(3 - step))

    def slot_rows(i):
        return pl.ds(PREFIX + (i // 4) * ROWS, ROWS)

    def reduce_a(h):
        for o in (1, 2, 3):
            for part in (1, 0):
                reduce_y(h, o, part).start()

    def reduce_b(h):
        for o in (1, 2, 3):
            reduce_y(h, o, 0).wait_recv()
            reduce_y(h, o, 1).wait_recv()
        for kv in range(2):
            far = acc[h, kv, slot_rows(0), :]
            mid = acc[h, kv, slot_rows(4), :]
            near = acc[h, kv, slot_rows(8), :]
            for o in (1, 2, 3):
                mid = mid + rrecv[h, o - 1, 0, kv].astype(jnp.float32)
                term = rrecv[h, o - 1, 1, kv].astype(jnp.float32)
                lower = jnp.where(y >= o, 1.0, 0.0).astype(jnp.float32)
                far = far + term * lower
                near = near + term * (1.0 - lower)
            zsend[h, 0, kv] = mid.astype(jnp.bfloat16)
            zsend[h, 1, kv] = far.astype(jnp.bfloat16)
            acc[h, kv, slot_rows(8), :] = near
        reduce_z(h, 1).start()
        reduce_z(h, 0).start()

    def reduce_c(h):
        reduce_z(h, 0).wait_recv()
        reduce_z(h, 1).wait_recv()
        for kv in range(2):
            near = acc[h, kv, slot_rows(8), :]
            for step in range(2):
                near = near + zrecv[h, step, kv].astype(jnp.float32)
            if kv == 0:
                near = near * SCALE
            okr[kv, h] = near.astype(jnp.bfloat16)

    def total_c(h):
        return send(csend.at[h], crecv.at[h], rc_s.at[h], rc_r.at[h], at_core)

    def total_x(h, o):
        return send(
            xsend.at[h, (x + o) % SIDE], xrecv.at[h, o - 1], rx_s.at[h, o - 1], rx_r.at[h, o - 1], at_x(o)
        )

    def total_y(h, o):
        return send(
            ysend.at[h, (y + o) % SIDE], yrecv.at[h, o - 1], rp_s.at[h, o - 1], rp_r.at[h, o - 1], at_y(o)
        )

    def total_z(h, o):
        return send(
            wsend.at[h, (z + o) % SIDE], wrecv.at[h, o - 1], rw_s.at[h, o - 1], rw_r.at[h, o - 1], at_z(o)
        )

    def total_a(h):
        csend[h] = acc[h, other, pl.ds(0, PREFIX), :].astype(jnp.bfloat16)
        total_c(h).start()

    def total_b(h):
        total_c(h).wait_recv()
        for i in range(SIDE):
            rows = pl.ds(256 * i, 256)
            both = acc[h, core, rows, :] + crecv[h, rows, :].astype(jnp.float32)
            acc[h, core, rows, :] = both
            xsend[h, i] = both.astype(jnp.bfloat16)
        for o in (1, 2, 3):
            total_x(h, o).start()

    def total_d(h):
        for o in (1, 2, 3):
            total_x(h, o).wait_recv()
        whole = acc[h, core, pl.ds(pl.multiple_of(x * 256, 256), 256), :]
        for o in (1, 2, 3):
            whole = whole + xrecv[h, o - 1].astype(jnp.float32)
        ysend[h] = whole.astype(jnp.bfloat16).reshape(SIDE, 64, DIM)
        ykept[h] = whole.reshape(SIDE, 64, DIM)
        for o in (1, 2, 3):
            total_y(h, o).start()

    def total_e(h):
        for o in (1, 2, 3):
            total_y(h, o).wait_recv()
        whole = ykept[h, y]
        for o in (1, 2, 3):
            whole = whole + yrecv[h, o - 1].astype(jnp.float32)
        wsend[h] = whole.reshape(SIDE, 16, DIM)
        for o in (1, 2, 3):
            total_z(h, o).start()

    def total_f(h):
        for o in (1, 2, 3):
            total_z(h, o).wait_recv()
        whole = wsend[h, z]
        for o in (1, 2, 3):
            whole = whole + wrecv[h, o - 1]
        whole = whole * jnp.where(core == 0, SCALE, 1.0).astype(jnp.float32)
        finall[smp, h] = whole.astype(jnp.bfloat16)

    def total_g(o):
        return send(finall.at[smp], finall.at[smp], rf_s.at[o - 1], rf_r.at[o - 1], smp_partners[o - 1])

    for part in range(2):
        for o in three:
            prefix_z(part, o).start()
    gather_a(0)
    gather_own(0)
    load_q.wait()
    load_do.wait()
    transpose_queries(q_v, qt)
    for part in range(2):
        for o in three:
            prefix_z(part, o).wait_recv()
        for o in three:
            prefix_y(part, o).start()
    gather_own(1)
    gather_a(1)
    transpose_queries(do_v, dot)
    for o in three:
        prefix_y(0, o).wait_recv()
    for o in three:
        prefix_x(0, o).start()
    gather_b(0)
    for o in three:
        prefix_y(1, o).wait_recv()
    for o in three:
        prefix_x(1, o).start()
    gather_own(2)
    gather_own(3)
    gather_a(2)
    prefix_last(0)
    gather_b(1)
    for h in range(2, HEADS):
        for o in three:
            prefix_x(h, o).start()
    gather_d(0)
    prefix_c(0).wait_recv()

    @pl.loop(0, HEADS)
    def _(h):
        @pl.when(h > 0)
        def _():
            gather_d(h)
            prefix_c(h).wait_recv()

        @pl.when(h == 0)
        def _():
            gather_a(3)

        transpose_keys(h, pre, win, kt, h)
        scores(h, 0, qt, dot, pre, win, bias, live, s_scr, dp_scr, pb, dsb, h)

        @pl.when(h > 0)
        def _():
            total_b(h - 1)

        @pl.when(h + 1 < HEADS)
        def _():
            prefix_last(h + 1)

        @pl.when(h + 2 < HEADS)
        def _():
            gather_b(h + 2)

        @pl.when(h > 1)
        def _():
            total_d(h - 2)
            reduce_b(h - 2)

        scores(h, 1, qt, dot, pre, win, bias, live, s_scr, dp_scr, pb, dsb, h)

        @pl.when(h > 2)
        def _():
            total_f(h - 3)

        prefix_terms(h, q_v, do_v, pb, dsb, acc, h)
        total_a(h)
        window_terms(h, q_v, do_v, pb, dsb, acc, rsend, h)
        reduce_a(h)

        @pl.when(h > 1)
        def _():
            total_e(h - 2)

        @pl.when(h > 2)
        def _():
            reduce_c(h - 3)

    query_terms(0, kt, dsb, dq_v, 0)
    total_d(2)
    total_b(3)
    reduce_b(2)
    query_terms(1, kt, dsb, dq_v, 1)
    query_terms(2, kt, dsb, dq_v, 2)
    total_f(1)
    total_e(2)
    query_terms(3, kt, dsb, dq_v, 3)
    store_q = pltpu.make_async_copy(dq_v, dq_hbm.at[0], local.at[12])
    store_q.start()
    total_d(3)
    reduce_b(3)
    reduce_c(1)
    total_e(3)
    total_f(2)
    reduce_c(2)
    total_f(3)
    for o in range(1, 8):
        total_g(o).start()
    reduce_c(3)
    stores = []
    for h in range(HEADS):
        cols = pl.ds(h * DIM, DIM)
        stores.append(pltpu.make_async_copy(okr.at[0, h], dkr_hbm.at[0, :, cols], local.at[2 * h]))
        stores.append(pltpu.make_async_copy(okr.at[1, h], dvr_hbm.at[0, :, cols], local.at[2 * h + 1]))
    for copy in stores:
        copy.start()
    for o in range(1, 8):
        total_g(o).wait_recv()
    for kv in range(2):
        for a in range(SIDE):
            for h in range(HEADS):
                okp[kv, pl.ds(16 * a, 16), pl.ds(h * DIM, DIM)] = finall[2 * a + kv, h]
    tail = [
        pltpu.make_async_copy(okp.at[0], dkp_hbm, local.at[8]),
        pltpu.make_async_copy(okp.at[1], dvp_hbm, local.at[9]),
    ]
    for copy in tail:
        copy.start()

    for o in three:
        for h in range(2):
            prefix_z(h, o).wait_send()
            prefix_y(h, o).wait_send()
    for o in range(1, 8):
        total_g(o).wait_send()

    @pl.loop(0, HEADS)
    def _(h):
        prefix_c(h).wait_send()
        total_c(h).wait_send()
        for step in range(2):
            gather_z(h, step).wait_send()
            reduce_z(h, step).wait_send()
        for o in (1, 2, 3):
            prefix_x(h, o).wait_send()
            total_x(h, o).wait_send()
            total_y(h, o).wait_send()
            total_z(h, o).wait_send()
            for part in range(2):
                gather_y(h, o, part).wait_send()
                reduce_y(h, o, part).wait_send()

    for copy in stores + tail + [store_q]:
        copy.wait()


def hand_over(*refs):
    ins, outs, held, sems = refs[:5], refs[5:10], refs[10:15], refs[15]
    first = [pltpu.make_async_copy(ins[i], held[i], sems.at[i]) for i in range(5)]
    second = [pltpu.make_async_copy(held[i], outs[i], sems.at[i]) for i in range(5)]
    for copy in first:
        copy.start()
    for a, b in zip(first, second):
        a.wait()
        b.start()
    for copy in second:
        copy.wait()


def shards(q, kp, vp, kr, vr, do, lengths, assign):
    bf, f32 = jnp.bfloat16, jnp.float32
    dma = pltpu.SemaphoreType.DMA
    hbm = pl.BlockSpec(memory_space=pl.ANY)
    smem = pl.BlockSpec(memory_space=pltpu.SMEM)
    H = HEADS
    outs = pl.pallas_call(
        kernel,
        out_shape=(
            jax.ShapeDtypeStruct(q.shape, bf),
            jax.ShapeDtypeStruct(kp.shape, bf),
            jax.ShapeDtypeStruct(vp.shape, bf),
            jax.ShapeDtypeStruct(kr.shape, bf),
            jax.ShapeDtypeStruct(vr.shape, bf),
        ),
        in_specs=[hbm] * 6 + [smem] * 2,
        out_specs=(hbm,) * 5,
        scratch_shapes=[
            pltpu.VMEM((ROWS, H * GROUP * DIM), bf),
            pltpu.VMEM((ROWS, H * GROUP * DIM), bf),
            pltpu.VMEM((ROWS, H * GROUP * DIM), bf),
            pltpu.VMEM((H, DIM, GROUP * ROWS), bf),
            pltpu.VMEM((H, DIM, GROUP * ROWS), bf),
            pltpu.VMEM((H, 2, PREFIX, DIM), bf),
            pltpu.VMEM((H, 2, 9, ROWS, DIM), bf),
            pltpu.VMEM((WINDOW, ROWS), f32),
            pltpu.VMEM((1, ROWS), f32),
            pltpu.VMEM((KEYS, QB), f32),
            pltpu.VMEM((KEYS, QB), f32),
            pltpu.VMEM((KEYS, GROUP * ROWS), bf),
            pltpu.VMEM((H, KEYS, GROUP * ROWS), bf),
            pltpu.VMEM((H, 2, KEPT, DIM), f32),
            pltpu.VMEM((H, DIM, KEYS), bf),
            pltpu.VMEM((H, 9, 2, ROWS, DIM), bf),
            pltpu.VMEM((H, 3, 2, 2, ROWS, DIM), bf),
            pltpu.VMEM((H, 2, 2, ROWS, DIM), bf),
            pltpu.VMEM((H, 2, 2, ROWS, DIM), bf),
            pltpu.VMEM((H, PREFIX, DIM), bf),
            pltpu.VMEM((H, PREFIX, DIM), bf),
            pltpu.VMEM((H, SIDE, 256, DIM), bf),
            pltpu.VMEM((H, 3, 256, DIM), bf),
            pltpu.VMEM((H, SIDE, 64, DIM), bf),
            pltpu.VMEM((H, SIDE, 64, DIM), f32),
            pltpu.VMEM((H, 3, 64, DIM), bf),
            pltpu.VMEM((H, SIDE, 16, DIM), f32),
            pltpu.VMEM((H, 3, 16, DIM), f32),
            pltpu.VMEM((8, H, 16, DIM), bf),
            pltpu.VMEM((2, H, ROWS, DIM), bf),
            pltpu.VMEM((2, 64, H * DIM), bf),
            dma((14,)),
            dma((H, 2)), dma((H, 2)), dma((H, 3, 2)), dma((H, 3, 2)),
            dma((2, 3)), dma((2, 3)), dma((2, 3)), dma((2, 3)),
            dma((H, 3)), dma((H, 3)), dma((H,)), dma((H,)),
            dma((H, 3, 2)), dma((H, 3, 2)), dma((H, 2)), dma((H, 2)),
            dma((H,)), dma((H,)), dma((H, 3)), dma((H, 3)),
            dma((H, 3)), dma((H, 3)), dma((H, 3)), dma((H, 3)),
            dma((7,)), dma((7,)),
        ],
        compiler_params=pltpu.CompilerParams(
            collective_id=0, has_side_effects=True, vmem_limit_bytes=63 * 1024 * 1024
        ),
        name="attention_backward",
    )(q, kp, vp, kr, vr, do, lengths, assign)
    return pl.pallas_call(
        hand_over,
        out_shape=tuple(jax.ShapeDtypeStruct(o.shape, o.dtype) for o in outs),
        in_specs=[hbm] * 5,
        out_specs=(hbm,) * 5,
        scratch_shapes=[pltpu.VMEM(o.shape, o.dtype) for o in outs] + [dma((5,))],
        compiler_params=pltpu.CompilerParams(vmem_limit_bytes=63 * 1024 * 1024),
        name="hand_over",
    )(*outs)


def solution(mesh):
    rows = P(("dp", "smp"), "ctx", None)
    prefix = P(("dp", "ctx"), None)
    return jax.shard_map(
        shards,
        mesh=mesh,
        in_specs=(rows, prefix, prefix, rows, rows, rows, P("dp"), P("dp")),
        out_specs=(rows, prefix, prefix, rows, rows),
        check_vma=False,
    )
```

```python
import functools

import jax
import jax.numpy as jnp
from jax import lax
from jax.experimental import pallas as pl
from jax.experimental.pallas import tpu as pltpu
from jax.sharding import PartitionSpec as P

HEADS = 4
GROUP = 8
DIM = 128
ROWS = 128
PREFIX = 1024
WINDOW = 9 * ROWS
KEYS = PREFIX + WINDOW
QB = 512
KEPT = PREFIX + 3 * ROWS
SIDE = 4
SCALE = DIM ** -0.5
LOG2E = 1.4426950408889634
MASKED = -1e30
RESPONSES = 16
MESH = pl.DeviceIdType.MESH


def dot_nt(a, b):
    return lax.dot_general(a, b, (((1,), (1,)), ((), ())), preferred_element_type=jnp.float32)


def dot_nn(a, b):
    return lax.dot_general(a, b, (((1,), (0,)), ((), ())), preferred_element_type=jnp.float32)


def fold(x, op):
    return op(x.reshape(x.shape[0] // 8, 8, x.shape[1]), axis=0)


def head_rows(kv, h, start, size, pre, win):
    if start < PREFIX:
        return pre[h, kv, pl.ds(start, size), :]
    i = (start - PREFIX) // ROWS
    return win[h, kv, i // 4, i % 4]


def stacked(ref, h):
    parts = [ref[:, pl.ds(pl.multiple_of(h * (GROUP * DIM) + i * DIM, DIM), DIM)] for i in range(GROUP)]
    return jnp.concatenate(parts, axis=0)


def scores(h, half, qt, dot, pre, win, bias, live, s_scr, dp_scr, pb, dsb, slot):
    cols = pl.ds(pl.multiple_of(half * QB, QB), QB)
    qs = qt[h, :, cols]
    gs = dot[h, :, cols]
    chunks = [(i, ROWS) for i in range(0, KEYS, ROWS)]
    factor = SCALE * LOG2E
    stats = []
    for start, size in chunks:
        s = dot_nn(head_rows(0, h, start, size, pre, win), qs)
        dp = dot_nn(head_rows(1, h, start, size, pre, win), gs)
        if start >= PREFIX:
            b = bias[pl.ds(start - PREFIX, size), :]
            s = s + jnp.concatenate([b] * (QB // ROWS), axis=1)
        top = fold(s, jnp.max) * factor
        p = jnp.exp2((s * factor).reshape(size // 8, 8, QB) - top[None]).reshape(size, QB)
        s_scr[pl.ds(start, size), :] = p
        dp_scr[pl.ds(start, size), :] = dp
        stats.append((top, fold(p, jnp.sum), fold(p * dp, jnp.sum)))
    whole = functools.reduce(jnp.maximum, [t for t, _, _ in stats])
    whole = jnp.max(whole, axis=0, keepdims=True)
    factors = [jnp.exp2(t - whole) for t, _, _ in stats]
    total = sum(t[1] * f for t, f in zip(stats, factors))
    dotted = sum(t[2] * f for t, f in zip(stats, factors))
    inverse = 1.0 / jnp.sum(total, axis=0, keepdims=True)
    delta = jnp.sum(dotted, axis=0, keepdims=True) * inverse
    live_row = live[...]
    inverse = inverse * jnp.concatenate([live_row] * (QB // ROWS), axis=1)
    for (start, size), f in zip(chunks, factors):
        rows = pl.ds(start, size)
        p = (s_scr[rows, :].reshape(size // 8, 8, QB) * (f * inverse)[None]).reshape(size, QB)
        pb[rows, cols] = p.astype(jnp.bfloat16)
        dsb[slot, rows, cols] = (p * (dp_scr[rows, :] - delta)).astype(jnp.bfloat16)


def prefix_terms(h, q_v, do_v, pb, dsb, acc, slot):
    rows = pl.ds(0, PREFIX)
    acc[h, 1, rows, :] = dot_nn(pb[rows, :], stacked(do_v, h))
    acc[h, 0, rows, :] = dot_nn(dsb[slot, rows, :], stacked(q_v, h))


def window_terms(h, q_v, do_v, pb, dsb, acc, rsend, slot):
    rows = pl.ds(PREFIX, WINDOW)
    for kv, term in ((1, dot_nn(pb[rows, :], stacked(do_v, h))), (0, dot_nn(dsb[slot, rows, :], stacked(q_v, h)))):
        for i in range(9):
            block = term[i * ROWS : (i + 1) * ROWS]
            rsend[h, i // 4, i % 4, kv] = block.astype(jnp.bfloat16)
            if i % 4 == 0:
                acc[h, kv, pl.ds(PREFIX + (i // 4) * ROWS, ROWS), :] = block


def query_terms(h, kt, dsb, dq_v, slot):
    dq = (dot_nn(kt[slot], dsb[slot]) * SCALE).T.astype(jnp.bfloat16)
    for i in range(GROUP):
        dq_v[:, pl.ds(pl.multiple_of(h * (GROUP * DIM) + i * DIM, DIM), DIM)] = dq[i * ROWS : (i + 1) * ROWS]


def transpose_keys(h, pre, win, kt, slot):
    for i in range(4):
        kt[slot, :, pl.ds(256 * i, 256)] = pre[h, 0, pl.ds(256 * i, 256), :].T
    for i in range(9):
        kt[slot, :, pl.ds(PREFIX + ROWS * i, ROWS)] = win[h, 0, i // 4, i % 4].T


def transpose_queries(ref, out):
    for h in range(HEADS):
        for i in range(GROUP):
            out[h, :, pl.ds(i * DIM, DIM)] = ref[:, pl.ds(h * (GROUP * DIM) + i * DIM, DIM)].T


def masks(place, smp, len_ref, asg_ref, bias, live):
    slot = place * ROWS + lax.broadcasted_iota(jnp.int32, (1, ROWS), 1)
    first = jnp.full((1, ROWS), 1 << 20, jnp.int32)
    start = jnp.int32(0)
    for r in range(RESPONSES):
        stop = start + jnp.where(asg_ref[r] == smp, len_ref[r], 0)
        first = jnp.where((slot >= start) & (slot < stop), start, first)
        start = stop
    live[...] = jnp.where(first < (1 << 20), 1.0, 0.0).astype(jnp.float32)
    for i in range(9):
        key = (place - 8 + i) * ROWS + lax.broadcasted_iota(jnp.int32, (ROWS, ROWS), 0)
        allowed = (key >= first) & (key <= slot)
        bias[pl.ds(i * ROWS, ROWS), :] = jnp.where(allowed, 0.0, MASKED).astype(jnp.float32)


def kernel(
    q_hbm, kp_hbm, vp_hbm, kr_hbm, vr_hbm, do_hbm, len_ref, asg_ref,
    dq_hbm, dkp_hbm, dvp_hbm, dkr_hbm, dvr_hbm,
    q_v, do_v, qt, dot, pre, win, bias, live, s_scr, dp_scr, pb, dsb, acc, kt,
    rsend, rrecv, zsend, zrecv,
    csend, crecv, xsend, xrecv, ysend, ykept, yrecv, wsend, wrecv, finall,
    okr, okp,
    local, gz_s, gz_r, gy_s, gy_r, pz_s, pz_r, py_s, py_r, px_s, px_r, pc_s, pc_r,
    ry_s, ry_r, rz_s, rz_r, rc_s, rc_r, rx_s, rx_r, rp_s, rp_r, rw_s, rw_r, rf_s, rf_r,
):
    ctx = lax.axis_index("ctx")
    smp = lax.axis_index("smp")
    z, y = ctx // SIDE, ctx % SIDE
    x, core = smp // 2, smp % 2
    other = 1 - core

    three = (1, 2, 3)

    def at_z(o):
        return {"ctx": ((z + o) % SIDE) * SIDE + y}

    def at_y(o):
        return {"ctx": z * SIDE + (y + o) % SIDE}

    def at_x(o):
        return {"smp": ((x + o) % SIDE) * 2 + core}

    at_core = {"smp": x * 2 + other}

    def send(src, dst, ss, rs, where):
        return pltpu.make_async_remote_copy(
            src_ref=src, dst_ref=dst, send_sem=ss, recv_sem=rs, device_id=where, device_id_type=MESH
        )

    barrier = pltpu.get_barrier_semaphore()
    partners = [at_z(o) for o in (1, 2, 3)] + [at_y(o) for o in (1, 2, 3)]
    smp_partners = [{"smp": (smp + o) % 8} for o in range(1, 8)]
    for where in partners + smp_partners:
        pl.semaphore_signal(barrier, inc=1, device_id=where, device_id_type=MESH)
    loads = []
    for h in range(HEADS):
        cols = pl.ds(h * DIM, DIM)
        loads.append(pltpu.make_async_copy(kr_hbm.at[0, :, cols], win.at[h, 0, 2, 0], local.at[2 * h]))
        loads.append(pltpu.make_async_copy(vr_hbm.at[0, :, cols], win.at[h, 1, 2, 0], local.at[2 * h + 1]))
    mine = pl.ds(pl.multiple_of(x * 256 + y * 64 + z * 16, 16), 16)
    from_rows = pl.ds(pl.multiple_of(x * 16, 16), 16)

    def load_prefix(h, src):
        return pltpu.make_async_copy(
            src.at[from_rows, pl.ds(h * DIM, DIM)], pre.at[h, core, mine, :], local.at[8 + h]
        )

    for copy in loads:
        copy.start()

    @pl.when(core == 0)
    def _():
        for h in range(HEADS):
            load_prefix(h, kp_hbm).start()

    @pl.when(core == 1)
    def _():
        for h in range(HEADS):
            load_prefix(h, vp_hbm).start()

    load_q = pltpu.make_async_copy(q_hbm.at[0], q_v, local.at[12])
    load_do = pltpu.make_async_copy(do_hbm.at[0], do_v, local.at[13])
    load_q.start()
    load_do.start()

    masks(ctx, smp, len_ref, asg_ref, bias, live)
    for copy in loads:
        copy.wait()
    for h in range(HEADS):
        load_prefix(h, kp_hbm).wait()
    pl.semaphore_wait(barrier, len(partners) + len(smp_partners))

    def gather_z(h, step):
        return send(win.at[h, :, 2, 0], win.at[h, :, 1 - step, 0], gz_s.at[h, step], gz_r.at[h, step], at_z(1 + step))

    def gather_y(h, o):
        later = jnp.where(y + o < SIDE, 1, 0)
        return send(
            win.at[h, :, pl.ds(later, 2), 0], win.at[h, :, pl.ds(0, 2), SIDE - o],
            gy_s.at[h, o - 1], gy_r.at[h, o - 1], at_y(o),
        )

    def gather_a(h):
        gather_z(h, 0).start()
        gather_z(h, 1).start()

    def gather_b(h):
        gather_z(h, 0).wait_recv()
        gather_z(h, 1).wait_recv()
        for o in three:
            gather_y(h, o).start()

    def gather_d(h):
        for o in (1, 2, 3):
            gather_y(h, o).wait_recv()

    def some(h):
        return pl.ds(0, 1) if h == 0 else pl.ds(1, HEADS - 1)

    def prefix_z(h, o):
        part = pre.at[some(h), core, mine, :]
        return send(part, part, pz_s.at[h, o - 1], pz_r.at[h, o - 1], at_z(o))

    def prefix_y(h, o):
        rows = pl.ds(pl.multiple_of(x * 256 + y * 64, 64), 64)
        part = pre.at[some(h), core, rows, :]
        return send(part, part, py_s.at[h, o - 1], py_r.at[h, o - 1], at_y(o))

    def prefix_x(h, o):
        rows = pl.ds(pl.multiple_of(x * 256, 256), 256)
        return send(
            pre.at[h, core, rows, :], pre.at[h, core, rows, :], px_s.at[h, o - 1], px_r.at[h, o - 1], at_x(o)
        )

    def prefix_c(h):
        return send(pre.at[h, core], pre.at[h, core], pc_s.at[h], pc_r.at[h], at_core)

    def prefix_last(h):
        for o in (1, 2, 3):
            prefix_x(h, o).wait_recv()
        prefix_c(h).start()

    def reduce_y(h, o):
        return send(
            rsend.at[h, pl.ds(0, 2), o], rrecv.at[h, o - 1], ry_s.at[h, o - 1], ry_r.at[h, o - 1], at_y(o)
        )

    def reduce_z(h, step):
        return send(zsend.at[h, step], zrecv.at[h, step], rz_s.at[h, step], rz_r.at[h, step], at_z(3 - step))

    def slot_rows(i):
        return pl.ds(PREFIX + (i // 4) * ROWS, ROWS)

    def reduce_a(h):
        for o in (1, 2, 3):
            reduce_y(h, o).start()

    def reduce_b(h):
        for o in (1, 2, 3):
            reduce_y(h, o).wait_recv()
        for kv in range(2):
            far = acc[h, kv, slot_rows(0), :]
            mid = acc[h, kv, slot_rows(4), :]
            near = acc[h, kv, slot_rows(8), :]
            for o in (1, 2, 3):
                one = rrecv[h, o - 1, 0, kv].astype(jnp.float32)
                two = rrecv[h, o - 1, 1, kv].astype(jnp.float32)
                lower = jnp.where(y >= o, 1.0, 0.0).astype(jnp.float32)
                far = far + one * lower
                near = near + two * (1.0 - lower)
                mid = mid + two * lower + one * (1.0 - lower)
            zsend[h, 0, kv] = mid.astype(jnp.bfloat16)
            zsend[h, 1, kv] = far.astype(jnp.bfloat16)
            acc[h, kv, slot_rows(8), :] = near
        reduce_z(h, 1).start()
        reduce_z(h, 0).start()

    def reduce_c(h):
        reduce_z(h, 0).wait_recv()
        reduce_z(h, 1).wait_recv()
        for kv in range(2):
            near = acc[h, kv, slot_rows(8), :]
            for step in range(2):
                near = near + zrecv[h, step, kv].astype(jnp.float32)
            if kv == 0:
                near = near * SCALE
            okr[kv, h] = near.astype(jnp.bfloat16)

    def total_c(h):
        return send(csend.at[h], crecv.at[h], rc_s.at[h], rc_r.at[h], at_core)

    def total_x(h, o):
        return send(
            xsend.at[h, (x + o) % SIDE], xrecv.at[h, o - 1], rx_s.at[h, o - 1], rx_r.at[h, o - 1], at_x(o)
        )

    def total_y(h, o):
        return send(
            ysend.at[h, (y + o) % SIDE], yrecv.at[h, o - 1], rp_s.at[h, o - 1], rp_r.at[h, o - 1], at_y(o)
        )

    def total_z(h, o):
        return send(
            wsend.at[h, (z + o) % SIDE], wrecv.at[h, o - 1], rw_s.at[h, o - 1], rw_r.at[h, o - 1], at_z(o)
        )

    def total_a(h):
        csend[h] = acc[h, other, pl.ds(0, PREFIX), :].astype(jnp.bfloat16)
        total_c(h).start()

    def total_b(h):
        total_c(h).wait_recv()
        for i in range(SIDE):
            rows = pl.ds(256 * i, 256)
            both = acc[h, core, rows, :] + crecv[h, rows, :].astype(jnp.float32)
            acc[h, core, rows, :] = both
            xsend[h, i] = both.astype(jnp.bfloat16)
        for o in (1, 2, 3):
            total_x(h, o).start()

    def total_d(h):
        for o in (1, 2, 3):
            total_x(h, o).wait_recv()
        whole = acc[h, core, pl.ds(pl.multiple_of(x * 256, 256), 256), :]
        for o in (1, 2, 3):
            whole = whole + xrecv[h, o - 1].astype(jnp.float32)
        ysend[h] = whole.astype(jnp.bfloat16).reshape(SIDE, 64, DIM)
        ykept[h] = whole.reshape(SIDE, 64, DIM)
        for o in (1, 2, 3):
            total_y(h, o).start()

    def total_e(h):
        for o in (1, 2, 3):
            total_y(h, o).wait_recv()
        whole = ykept[h, y]
        for o in (1, 2, 3):
            whole = whole + yrecv[h, o - 1].astype(jnp.float32)
        wsend[h] = whole.reshape(SIDE, 16, DIM)
        for o in (1, 2, 3):
            total_z(h, o).start()

    def total_f(h):
        for o in (1, 2, 3):
            total_z(h, o).wait_recv()
        whole = wsend[h, z]
        for o in (1, 2, 3):
            whole = whole + wrecv[h, o - 1]
        whole = whole * jnp.where(core == 0, SCALE, 1.0).astype(jnp.float32)
        finall[smp, h] = whole.astype(jnp.bfloat16)

    def total_g(o):
        return send(finall.at[smp], finall.at[smp], rf_s.at[o - 1], rf_r.at[o - 1], smp_partners[o - 1])

    for part in range(2):
        for o in three:
            prefix_z(part, o).start()
    gather_a(0)
    load_q.wait()
    load_do.wait()
    transpose_queries(q_v, qt)
    for part in range(2):
        for o in three:
            prefix_z(part, o).wait_recv()
        for o in three:
            prefix_y(part, o).start()
    gather_a(1)
    transpose_queries(do_v, dot)
    for o in three:
        prefix_y(0, o).wait_recv()
    for o in three:
        prefix_x(0, o).start()
    gather_b(0)
    for o in three:
        prefix_y(1, o).wait_recv()
    for o in three:
        prefix_x(1, o).start()
    gather_a(2)
    prefix_last(0)
    gather_b(1)
    for h in range(2, HEADS):
        for o in three:
            prefix_x(h, o).start()
    gather_d(0)
    prefix_c(0).wait_recv()

    @pl.loop(0, 2 * HEADS)
    def _(it):
        h, half = it // 2, it % 2

        @pl.when(half == 0)
        def _():
            @pl.when(h > 0)
            def _():
                gather_d(h)
                prefix_c(h).wait_recv()

            @pl.when(h == 0)
            def _():
                gather_a(3)

            transpose_keys(h, pre, win, kt, h)

        scores(h, half, qt, dot, pre, win, bias, live, s_scr, dp_scr, pb, dsb, h)

        @pl.when(half == 0)
        def _():
            @pl.when(h > 0)
            def _():
                total_b(h - 1)

            @pl.when(h + 1 < HEADS)
            def _():
                prefix_last(h + 1)

            @pl.when(h + 2 < HEADS)
            def _():
                gather_b(h + 2)

            @pl.when(h > 1)
            def _():
                total_d(h - 2)
                reduce_b(h - 2)

        @pl.when(half == 1)
        def _():
            prefix_terms(h, q_v, do_v, pb, dsb, acc, h)
            total_a(h)
            window_terms(h, q_v, do_v, pb, dsb, acc, rsend, h)
            reduce_a(h)

            @pl.when(h == HEADS - 1)
            def _():
                total_b(h)

            @pl.when(h > 2)
            def _():
                total_f(h - 3)

            @pl.when(h > 1)
            def _():
                total_e(h - 2)

            @pl.when(h > 2)
            def _():
                reduce_c(h - 3)

    total_d(2)
    query_terms(0, kt, dsb, q_v, 0)
    reduce_b(2)
    query_terms(1, kt, dsb, q_v, 1)
    query_terms(2, kt, dsb, q_v, 2)
    total_e(2)
    query_terms(3, kt, dsb, q_v, 3)
    store_q = pltpu.make_async_copy(q_v, dq_hbm.at[0], local.at[12])
    store_q.start()
    total_d(3)
    total_f(1)
    for o in three:
        for h in range(2):
            prefix_z(h, o).wait_send()
            prefix_y(h, o).wait_send()
    reduce_b(3)
    reduce_c(1)

    @pl.loop(0, HEADS)
    def _(h):
        prefix_c(h).wait_send()
        for step in range(2):
            gather_z(h, step).wait_send()
        for o in three:
            prefix_x(h, o).wait_send()
            gather_y(h, o).wait_send()

    total_e(3)
    total_f(2)
    reduce_c(2)

    @pl.loop(0, HEADS)
    def _(h):
        total_c(h).wait_send()
        for step in range(2):
            reduce_z(h, step).wait_send()
        for o in three:
            total_x(h, o).wait_send()
            total_y(h, o).wait_send()
            reduce_y(h, o).wait_send()

    total_f(3)
    for o in range(1, 8):
        total_g(o).start()
    reduce_c(3)
    stores = []
    for h in range(HEADS):
        cols = pl.ds(h * DIM, DIM)
        stores.append(pltpu.make_async_copy(okr.at[0, h], dkr_hbm.at[0, :, cols], local.at[2 * h]))
        stores.append(pltpu.make_async_copy(okr.at[1, h], dvr_hbm.at[0, :, cols], local.at[2 * h + 1]))
    for copy in stores:
        copy.start()
    for o in range(1, 8):
        total_g(o).wait_recv()
    for kv in range(2):
        for a in range(SIDE):
            for h in range(HEADS):
                okp[kv, pl.ds(16 * a, 16), pl.ds(h * DIM, DIM)] = finall[2 * a + kv, h]
    tail = [
        pltpu.make_async_copy(okp.at[0], dkp_hbm, local.at[8]),
        pltpu.make_async_copy(okp.at[1], dvp_hbm, local.at[9]),
    ]
    for copy in tail:
        copy.start()

    for o in range(1, 8):
        total_g(o).wait_send()

    @pl.loop(0, HEADS)
    def _(h):
        for o in three:
            total_z(h, o).wait_send()

    for copy in stores + tail + [store_q]:
        copy.wait()


def hand_over(*refs):
    ins, outs, held, sems = refs[:5], refs[5:10], refs[10:15], refs[15]
    first = [pltpu.make_async_copy(ins[i], held[i], sems.at[i]) for i in range(5)]
    second = [pltpu.make_async_copy(held[i], outs[i], sems.at[i]) for i in range(5)]
    for copy in first:
        copy.start()
    for a, b in zip(first, second):
        a.wait()
        b.start()
    for copy in second:
        copy.wait()


def shards(q, kp, vp, kr, vr, do, lengths, assign):
    bf, f32 = jnp.bfloat16, jnp.float32
    dma = pltpu.SemaphoreType.DMA
    hbm = pl.BlockSpec(memory_space=pl.ANY)
    smem = pl.BlockSpec(memory_space=pltpu.SMEM)
    H = HEADS
    outs = pl.pallas_call(
        kernel,
        out_shape=(
            jax.ShapeDtypeStruct(q.shape, bf),
            jax.ShapeDtypeStruct(kp.shape, bf),
            jax.ShapeDtypeStruct(vp.shape, bf),
            jax.ShapeDtypeStruct(kr.shape, bf),
            jax.ShapeDtypeStruct(vr.shape, bf),
        ),
        in_specs=[hbm] * 6 + [smem] * 2,
        out_specs=(hbm,) * 5,
        scratch_shapes=[
            pltpu.VMEM((ROWS, H * GROUP * DIM), bf),
            pltpu.VMEM((ROWS, H * GROUP * DIM), bf),
            pltpu.VMEM((H, DIM, GROUP * ROWS), bf),
            pltpu.VMEM((H, DIM, GROUP * ROWS), bf),
            pltpu.VMEM((H, 2, PREFIX, DIM), bf),
            pltpu.VMEM((H, 2, 3, 4, ROWS, DIM), bf),
            pltpu.VMEM((WINDOW, ROWS), f32),
            pltpu.VMEM((1, ROWS), f32),
            pltpu.VMEM((KEYS, QB), f32),
            pltpu.VMEM((KEYS, QB), f32),
            pltpu.VMEM((KEYS, GROUP * ROWS), bf),
            pltpu.VMEM((H, KEYS, GROUP * ROWS), bf),
            pltpu.VMEM((H, 2, KEPT, DIM), f32),
            pltpu.VMEM((H, DIM, KEYS), bf),
            pltpu.VMEM((H, 3, 4, 2, ROWS, DIM), bf),
            pltpu.VMEM((H, 3, 2, 2, ROWS, DIM), bf),
            pltpu.VMEM((H, 2, 2, ROWS, DIM), bf),
            pltpu.VMEM((H, 2, 2, ROWS, DIM), bf),
            pltpu.VMEM((H, PREFIX, DIM), bf),
            pltpu.VMEM((H, PREFIX, DIM), bf),
            pltpu.VMEM((H, SIDE, 256, DIM), bf),
            pltpu.VMEM((H, 3, 256, DIM), bf),
            pltpu.VMEM((H, SIDE, 64, DIM), bf),
            pltpu.VMEM((H, SIDE, 64, DIM), f32),
            pltpu.VMEM((H, 3, 64, DIM), bf),
            pltpu.VMEM((H, SIDE, 16, DIM), f32),
            pltpu.VMEM((H, 3, 16, DIM), f32),
            pltpu.VMEM((8, H, 16, DIM), bf),
            pltpu.VMEM((2, H, ROWS, DIM), bf),
            pltpu.VMEM((2, 64, H * DIM), bf),
            dma((14,)),
            dma((H, 2)), dma((H, 2)), dma((H, 3)), dma((H, 3)),
            dma((2, 3)), dma((2, 3)), dma((2, 3)), dma((2, 3)),
            dma((H, 3)), dma((H, 3)), dma((H,)), dma((H,)),
            dma((H, 3)), dma((H, 3)), dma((H, 2)), dma((H, 2)),
            dma((H,)), dma((H,)), dma((H, 3)), dma((H, 3)),
            dma((H, 3)), dma((H, 3)), dma((H, 3)), dma((H, 3)),
            dma((7,)), dma((7,)),
        ],
        compiler_params=pltpu.CompilerParams(
            collective_id=0, has_side_effects=True, vmem_limit_bytes=63 * 1024 * 1024
        ),
        name="attention_backward",
    )(q, kp, vp, kr, vr, do, lengths, assign)
    return pl.pallas_call(
        hand_over,
        out_shape=tuple(jax.ShapeDtypeStruct(o.shape, o.dtype) for o in outs),
        in_specs=[hbm] * 5,
        out_specs=(hbm,) * 5,
        scratch_shapes=[pltpu.VMEM(o.shape, o.dtype) for o in outs] + [dma((5,))],
        compiler_params=pltpu.CompilerParams(vmem_limit_bytes=63 * 1024 * 1024),
        name="hand_over",
    )(*outs)


def solution(mesh):
    rows = P(("dp", "smp"), "ctx", None)
    prefix = P(("dp", "ctx"), None)
    return jax.shard_map(
        shards,
        mesh=mesh,
        in_specs=(rows, prefix, prefix, rows, rows, rows, P("dp"), P("dp")),
        out_specs=(rows, prefix, prefix, rows, rows),
        check_vma=False,
    )
```

```python
import functools

import jax
import jax.numpy as jnp
from jax import lax
from jax.experimental import pallas as pl
from jax.experimental.pallas import tpu as pltpu
from jax.sharding import PartitionSpec as P

HEADS = 4
GROUP = 8
DIM = 128
ROWS = 128
PREFIX = 1024
WINDOW = 9 * ROWS
KEYS = PREFIX + WINDOW
QB = 512
KEPT = PREFIX + 3 * ROWS
SIDE = 4
SCALE = DIM ** -0.5
LOG2E = 1.4426950408889634
MASKED = -1e30
RESPONSES = 16
MESH = pl.DeviceIdType.MESH


def dot_nt(a, b):
    return lax.dot_general(a, b, (((1,), (1,)), ((), ())), preferred_element_type=jnp.float32)


def dot_nn(a, b):
    return lax.dot_general(a, b, (((1,), (0,)), ((), ())), preferred_element_type=jnp.float32)


def fold(x, op):
    return op(x.reshape(x.shape[0] // 8, 8, x.shape[1]), axis=0)


def head_rows(kv, h, start, size, pre, win):
    if start < PREFIX:
        return pre[h, kv, pl.ds(start, size), :]
    i = (start - PREFIX) // ROWS
    return win[h, kv, i // 4, i % 4]


def stacked(ref, h):
    parts = [ref[:, pl.ds(pl.multiple_of(h * (GROUP * DIM) + i * DIM, DIM), DIM)] for i in range(GROUP)]
    return jnp.concatenate(parts, axis=0)


def scores(h, half, qt, dot, pre, win, bias, live, s_scr, dp_scr, pb, dsb, slot):
    cols = pl.ds(pl.multiple_of(half * QB, QB), QB)
    qs = qt[h, :, cols]
    gs = dot[h, :, cols]
    chunks = [(i, ROWS) for i in range(0, KEYS, ROWS)]
    factor = SCALE * LOG2E
    stats = []
    for start, size in chunks:
        s = dot_nn(head_rows(0, h, start, size, pre, win), qs)
        dp = dot_nn(head_rows(1, h, start, size, pre, win), gs)
        if start >= PREFIX:
            b = bias[pl.ds(start - PREFIX, size), :]
            s = s + jnp.concatenate([b] * (QB // ROWS), axis=1)
        top = fold(s, jnp.max) * factor
        p = jnp.exp2((s * factor).reshape(size // 8, 8, QB) - top[None]).reshape(size, QB)
        s_scr[pl.ds(start, size), :] = p
        dp_scr[pl.ds(start, size), :] = dp
        stats.append((top, fold(p, jnp.sum), fold(p * dp, jnp.sum)))
    whole = functools.reduce(jnp.maximum, [t for t, _, _ in stats])
    whole = jnp.max(whole, axis=0, keepdims=True)
    factors = [jnp.exp2(t - whole) for t, _, _ in stats]
    total = sum(t[1] * f for t, f in zip(stats, factors))
    dotted = sum(t[2] * f for t, f in zip(stats, factors))
    inverse = 1.0 / jnp.sum(total, axis=0, keepdims=True)
    delta = jnp.sum(dotted, axis=0, keepdims=True) * inverse
    live_row = live[...]
    inverse = inverse * jnp.concatenate([live_row] * (QB // ROWS), axis=1)
    for (start, size), f in zip(chunks, factors):
        rows = pl.ds(start, size)
        p = (s_scr[rows, :].reshape(size // 8, 8, QB) * (f * inverse)[None]).reshape(size, QB)
        pb[rows, cols] = p.astype(jnp.bfloat16)
        dsb[slot, rows, cols] = (p * (dp_scr[rows, :] - delta)).astype(jnp.bfloat16)


def prefix_terms(h, q_v, do_v, pb, dsb, acc, slot):
    rows = pl.ds(0, PREFIX)
    acc[h, 1, rows, :] = dot_nn(pb[rows, :], stacked(do_v, h))
    acc[h, 0, rows, :] = dot_nn(dsb[slot, rows, :], stacked(q_v, h))


def window_terms(h, q_v, do_v, pb, dsb, acc, rsend, slot):
    rows = pl.ds(PREFIX, WINDOW)
    for kv, term in ((1, dot_nn(pb[rows, :], stacked(do_v, h))), (0, dot_nn(dsb[slot, rows, :], stacked(q_v, h)))):
        for i in range(9):
            block = term[i * ROWS : (i + 1) * ROWS]
            rsend[h, i // 4, i % 4, kv] = block.astype(jnp.bfloat16)
            if i % 4 == 0:
                acc[h, kv, pl.ds(PREFIX + (i // 4) * ROWS, ROWS), :] = block


def query_terms(h, kt, dsb, dq_v, slot):
    dq = (dot_nn(kt[slot], dsb[slot]) * SCALE).T.astype(jnp.bfloat16)
    for i in range(GROUP):
        dq_v[:, pl.ds(pl.multiple_of(h * (GROUP * DIM) + i * DIM, DIM), DIM)] = dq[i * ROWS : (i + 1) * ROWS]


def transpose_keys(h, pre, win, kt, slot):
    for i in range(4):
        kt[slot, :, pl.ds(256 * i, 256)] = pre[h, 0, pl.ds(256 * i, 256), :].T
    for i in range(9):
        kt[slot, :, pl.ds(PREFIX + ROWS * i, ROWS)] = win[h, 0, i // 4, i % 4].T


def transpose_queries(ref, out):
    for h in range(HEADS):
        for i in range(GROUP):
            out[h, :, pl.ds(i * DIM, DIM)] = ref[:, pl.ds(h * (GROUP * DIM) + i * DIM, DIM)].T


def masks(place, smp, len_ref, asg_ref, bias, live):
    slot = place * ROWS + lax.broadcasted_iota(jnp.int32, (1, ROWS), 1)
    first = jnp.full((1, ROWS), 1 << 20, jnp.int32)
    start = jnp.int32(0)
    for r in range(RESPONSES):
        stop = start + jnp.where(asg_ref[r] == smp, len_ref[r], 0)
        first = jnp.where((slot >= start) & (slot < stop), start, first)
        start = stop
    live[...] = jnp.where(first < (1 << 20), 1.0, 0.0).astype(jnp.float32)
    for i in range(9):
        key = (place - 8 + i) * ROWS + lax.broadcasted_iota(jnp.int32, (ROWS, ROWS), 0)
        allowed = (key >= first) & (key <= slot)
        bias[pl.ds(i * ROWS, ROWS), :] = jnp.where(allowed, 0.0, MASKED).astype(jnp.float32)


def kernel(
    q_hbm, kp_hbm, vp_hbm, kr_hbm, vr_hbm, do_hbm, len_ref, asg_ref,
    dq_hbm, dkp_hbm, dvp_hbm, dkr_hbm, dvr_hbm,
    q_v, do_v, qt, dot, pre, win, bias, live, s_scr, dp_scr, pb, dsb, acc, kt,
    rsend, rrecv, zsend, zrecv,
    csend, crecv, xsend, xrecv, ysend, ykept, yrecv, wsend, wrecv, finall,
    okr, okp,
    local, gz_s, gz_r, gy_s, gy_r, pz_s, pz_r, py_s, py_r, px_s, px_r, pc_s, pc_r,
    ry_s, ry_r, rz_s, rz_r, rc_s, rc_r, rx_s, rx_r, rp_s, rp_r, rw_s, rw_r, rf_s, rf_r,
):
    ctx = lax.axis_index("ctx")
    smp = lax.axis_index("smp")
    z, y = ctx // SIDE, ctx % SIDE
    x, core = smp // 2, smp % 2
    other = 1 - core

    three = (1, 2, 3)

    def at_z(o):
        return {"ctx": ((z + o) % SIDE) * SIDE + y}

    def at_y(o):
        return {"ctx": z * SIDE + (y + o) % SIDE}

    def at_x(o):
        return {"smp": ((x + o) % SIDE) * 2 + core}

    at_core = {"smp": x * 2 + other}

    def send(src, dst, ss, rs, where):
        return pltpu.make_async_remote_copy(
            src_ref=src, dst_ref=dst, send_sem=ss, recv_sem=rs, device_id=where, device_id_type=MESH
        )

    barrier = pltpu.get_barrier_semaphore()
    partners = [at_z(o) for o in (1, 2, 3)] + [at_y(o) for o in (1, 2, 3)]
    smp_partners = [{"smp": (smp + o) % 8} for o in range(1, 8)]
    for where in partners + smp_partners:
        pl.semaphore_signal(barrier, inc=1, device_id=where, device_id_type=MESH)
    loads = []
    for h in range(HEADS):
        cols = pl.ds(h * DIM, DIM)
        loads.append(pltpu.make_async_copy(kr_hbm.at[0, :, cols], win.at[h, 0, 2, 0], local.at[2 * h]))
        loads.append(pltpu.make_async_copy(vr_hbm.at[0, :, cols], win.at[h, 1, 2, 0], local.at[2 * h + 1]))
    mine = pl.ds(pl.multiple_of(x * 256 + y * 64 + z * 16, 16), 16)
    from_rows = pl.ds(pl.multiple_of(x * 16, 16), 16)

    def load_prefix(h, src):
        return pltpu.make_async_copy(
            src.at[from_rows, pl.ds(h * DIM, DIM)], pre.at[h, core, mine, :], local.at[8 + h]
        )

    for copy in loads:
        copy.start()

    @pl.when(core == 0)
    def _():
        for h in range(HEADS):
            load_prefix(h, kp_hbm).start()

    @pl.when(core == 1)
    def _():
        for h in range(HEADS):
            load_prefix(h, vp_hbm).start()

    load_q = pltpu.make_async_copy(q_hbm.at[0], q_v, local.at[12])
    load_do = pltpu.make_async_copy(do_hbm.at[0], do_v, local.at[13])
    load_q.start()
    load_do.start()

    masks(ctx, smp, len_ref, asg_ref, bias, live)
    for copy in loads:
        copy.wait()
    for h in range(HEADS):
        load_prefix(h, kp_hbm).wait()
    pl.semaphore_wait(barrier, len(partners) + len(smp_partners))

    def gather_z(h, step):
        return send(win.at[h, :, 2, 0], win.at[h, :, 1 - step, 0], gz_s.at[h, step], gz_r.at[h, step], at_z(1 + step))

    def gather_y(h, o):
        later = jnp.where(y + o < SIDE, 1, 0)
        return send(
            win.at[h, :, pl.ds(later, 2), 0], win.at[h, :, pl.ds(0, 2), SIDE - o],
            gy_s.at[h, o - 1], gy_r.at[h, o - 1], at_y(o),
        )

    def gather_a(h):
        gather_z(h, 0).start()
        gather_z(h, 1).start()

    def gather_b(h):
        gather_z(h, 0).wait_recv()
        gather_z(h, 1).wait_recv()
        for o in three:
            gather_y(h, o).start()

    def gather_d(h):
        for o in (1, 2, 3):
            gather_y(h, o).wait_recv()

    def some(h):
        return pl.ds(0, 1) if h == 0 else pl.ds(1, HEADS - 1)

    def prefix_z(h, o):
        part = pre.at[some(h), core, mine, :]
        return send(part, part, pz_s.at[h, o - 1], pz_r.at[h, o - 1], at_z(o))

    def prefix_y(h, o):
        rows = pl.ds(pl.multiple_of(x * 256 + y * 64, 64), 64)
        part = pre.at[some(h), core, rows, :]
        return send(part, part, py_s.at[h, o - 1], py_r.at[h, o - 1], at_y(o))

    def prefix_x(h, o):
        rows = pl.ds(pl.multiple_of(x * 256, 256), 256)
        return send(
            pre.at[h, core, rows, :], pre.at[h, core, rows, :], px_s.at[h, o - 1], px_r.at[h, o - 1], at_x(o)
        )

    def prefix_c(h):
        return send(pre.at[h, core], pre.at[h, core], pc_s.at[h], pc_r.at[h], at_core)

    def prefix_last(h):
        for o in (1, 2, 3):
            prefix_x(h, o).wait_recv()
        prefix_c(h).start()

    def reduce_y(h, o):
        return send(
            rsend.at[h, pl.ds(0, 2), o], rrecv.at[h, o - 1], ry_s.at[h, o - 1], ry_r.at[h, o - 1], at_y(o)
        )

    def reduce_z(h, step):
        return send(zsend.at[h, step], zrecv.at[h, step], rz_s.at[h, step], rz_r.at[h, step], at_z(3 - step))

    def slot_rows(i):
        return pl.ds(PREFIX + (i // 4) * ROWS, ROWS)

    def reduce_a(h):
        for o in (1, 2, 3):
            reduce_y(h, o).start()

    def reduce_b(h):
        for o in (1, 2, 3):
            reduce_y(h, o).wait_recv()
        for kv in range(2):
            far = acc[h, kv, slot_rows(0), :]
            mid = acc[h, kv, slot_rows(4), :]
            near = acc[h, kv, slot_rows(8), :]
            for o in (1, 2, 3):
                one = rrecv[h, o - 1, 0, kv].astype(jnp.float32)
                two = rrecv[h, o - 1, 1, kv].astype(jnp.float32)
                lower = jnp.where(y >= o, 1.0, 0.0).astype(jnp.float32)
                far = far + one * lower
                near = near + two * (1.0 - lower)
                mid = mid + two * lower + one * (1.0 - lower)
            zsend[h, 0, kv] = mid.astype(jnp.bfloat16)
            zsend[h, 1, kv] = far.astype(jnp.bfloat16)
            acc[h, kv, slot_rows(8), :] = near
        reduce_z(h, 1).start()
        reduce_z(h, 0).start()

    def reduce_c(h):
        reduce_z(h, 0).wait_recv()
        reduce_z(h, 1).wait_recv()
        for kv in range(2):
            near = acc[h, kv, slot_rows(8), :]
            for step in range(2):
                near = near + zrecv[h, step, kv].astype(jnp.float32)
            if kv == 0:
                near = near * SCALE
            okr[kv, h] = near.astype(jnp.bfloat16)

    def total_c(h):
        return send(csend.at[h], crecv.at[h], rc_s.at[h], rc_r.at[h], at_core)

    def total_x(h, o):
        return send(
            xsend.at[h, (x + o) % SIDE], xrecv.at[h, o - 1], rx_s.at[h, o - 1], rx_r.at[h, o - 1], at_x(o)
        )

    def total_y(h, o):
        return send(
            ysend.at[h, (y + o) % SIDE], yrecv.at[h, o - 1], rp_s.at[h, o - 1], rp_r.at[h, o - 1], at_y(o)
        )

    def total_z(h, o):
        return send(
            wsend.at[h, (z + o) % SIDE], wrecv.at[h, o - 1], rw_s.at[h, o - 1], rw_r.at[h, o - 1], at_z(o)
        )

    def total_a(h):
        csend[h] = acc[h, other, pl.ds(0, PREFIX), :].astype(jnp.bfloat16)
        total_c(h).start()

    def total_b(h):
        total_c(h).wait_recv()
        for i in range(SIDE):
            rows = pl.ds(256 * i, 256)
            both = acc[h, core, rows, :] + crecv[h, rows, :].astype(jnp.float32)
            acc[h, core, rows, :] = both
            xsend[h, i] = both.astype(jnp.bfloat16)
        for o in (1, 2, 3):
            total_x(h, o).start()

    def total_d(h):
        for o in (1, 2, 3):
            total_x(h, o).wait_recv()
        whole = acc[h, core, pl.ds(pl.multiple_of(x * 256, 256), 256), :]
        for o in (1, 2, 3):
            whole = whole + xrecv[h, o - 1].astype(jnp.float32)
        ysend[h] = whole.astype(jnp.bfloat16).reshape(SIDE, 64, DIM)
        ykept[h] = whole.reshape(SIDE, 64, DIM)
        for o in (1, 2, 3):
            total_y(h, o).start()

    def total_e(h):
        for o in (1, 2, 3):
            total_y(h, o).wait_recv()
        whole = ykept[h, y]
        for o in (1, 2, 3):
            whole = whole + yrecv[h, o - 1].astype(jnp.float32)
        wsend[h] = whole.reshape(SIDE, 16, DIM)
        for o in (1, 2, 3):
            total_z(h, o).start()

    def total_f(h):
        for o in (1, 2, 3):
            total_z(h, o).wait_recv()
        whole = wsend[h, z]
        for o in (1, 2, 3):
            whole = whole + wrecv[h, o - 1]
        whole = whole * jnp.where(core == 0, SCALE, 1.0).astype(jnp.float32)
        finall[smp, h] = whole.astype(jnp.bfloat16)

    def total_g(o):
        return send(finall.at[smp], finall.at[smp], rf_s.at[o - 1], rf_r.at[o - 1], smp_partners[o - 1])

    for part in range(2):
        for o in three:
            prefix_z(part, o).start()
    gather_a(0)
    load_q.wait()
    load_do.wait()
    transpose_queries(q_v, qt)
    for part in range(2):
        for o in three:
            prefix_z(part, o).wait_recv()
        for o in three:
            prefix_y(part, o).start()
    gather_a(1)
    transpose_queries(do_v, dot)
    for o in three:
        prefix_y(0, o).wait_recv()
    for o in three:
        prefix_x(0, o).start()
    gather_b(0)
    for o in three:
        prefix_y(1, o).wait_recv()
    for o in three:
        prefix_x(1, o).start()
    gather_a(2)
    prefix_last(0)
    gather_b(1)
    for h in range(2, HEADS):
        for o in three:
            prefix_x(h, o).start()
    gather_d(0)
    prefix_c(0).wait_recv()

    @pl.loop(0, 2 * HEADS)
    def _(it):
        h, half = it // 2, it % 2

        @pl.when(half == 0)
        def _():
            @pl.when(h > 0)
            def _():
                gather_d(h)
                prefix_c(h).wait_recv()

            @pl.when(h == 0)
            def _():
                gather_a(3)

        scores(h, half, qt, dot, pre, win, bias, live, s_scr, dp_scr, pb, dsb, h)

        @pl.when(half == 0)
        def _():
            @pl.when(h > 0)
            def _():
                total_b(h - 1)

            @pl.when(h + 1 < HEADS)
            def _():
                prefix_last(h + 1)

            @pl.when(h + 2 < HEADS)
            def _():
                gather_b(h + 2)

            @pl.when(h > 1)
            def _():
                total_d(h - 2)
                reduce_b(h - 2)

        @pl.when(half == 1)
        def _():
            prefix_terms(h, q_v, do_v, pb, dsb, acc, h)
            total_a(h)
            window_terms(h, q_v, do_v, pb, dsb, acc, rsend, h)
            reduce_a(h)

            @pl.when(h == HEADS - 1)
            def _():
                total_b(h)

            @pl.when(h > 2)
            def _():
                total_f(h - 3)

            @pl.when(h > 1)
            def _():
                total_e(h - 2)

            @pl.when(h > 2)
            def _():
                reduce_c(h - 3)

    total_d(2)
    transpose_keys(0, pre, win, kt, 0)
    query_terms(0, kt, dsb, q_v, 0)
    reduce_b(2)
    transpose_keys(1, pre, win, kt, 1)
    query_terms(1, kt, dsb, q_v, 1)
    transpose_keys(2, pre, win, kt, 2)
    query_terms(2, kt, dsb, q_v, 2)
    total_e(2)
    total_d(3)
    transpose_keys(3, pre, win, kt, 3)
    query_terms(3, kt, dsb, q_v, 3)
    store_q = pltpu.make_async_copy(q_v, dq_hbm.at[0], local.at[12])
    store_q.start()
    total_f(1)
    for o in three:
        for h in range(2):
            prefix_z(h, o).wait_send()
            prefix_y(h, o).wait_send()
    reduce_b(3)
    reduce_c(1)

    @pl.loop(0, HEADS)
    def _(h):
        prefix_c(h).wait_send()
        for step in range(2):
            gather_z(h, step).wait_send()
        for o in three:
            prefix_x(h, o).wait_send()
            gather_y(h, o).wait_send()

    total_e(3)
    total_f(2)
    reduce_c(2)

    @pl.loop(0, HEADS)
    def _(h):
        total_c(h).wait_send()
        for step in range(2):
            reduce_z(h, step).wait_send()
        for o in three:
            total_x(h, o).wait_send()
            total_y(h, o).wait_send()
            reduce_y(h, o).wait_send()

    total_f(3)
    for o in range(1, 8):
        total_g(o).start()
    reduce_c(3)
    stores = []
    for h in range(HEADS):
        cols = pl.ds(h * DIM, DIM)
        stores.append(pltpu.make_async_copy(okr.at[0, h], dkr_hbm.at[0, :, cols], local.at[2 * h]))
        stores.append(pltpu.make_async_copy(okr.at[1, h], dvr_hbm.at[0, :, cols], local.at[2 * h + 1]))
    for copy in stores:
        copy.start()
    for o in range(1, 8):
        total_g(o).wait_recv()
    for kv in range(2):
        for a in range(SIDE):
            for h in range(HEADS):
                okp[kv, pl.ds(16 * a, 16), pl.ds(h * DIM, DIM)] = finall[2 * a + kv, h]
    tail = [
        pltpu.make_async_copy(okp.at[0], dkp_hbm, local.at[8]),
        pltpu.make_async_copy(okp.at[1], dvp_hbm, local.at[9]),
    ]
    for copy in tail:
        copy.start()

    for o in range(1, 8):
        total_g(o).wait_send()

    @pl.loop(0, HEADS)
    def _(h):
        for o in three:
            total_z(h, o).wait_send()

    for copy in stores + tail + [store_q]:
        copy.wait()


def hand_over(*refs):
    ins, outs, held, sems = refs[:5], refs[5:10], refs[10:15], refs[15]
    first = [pltpu.make_async_copy(ins[i], held[i], sems.at[i]) for i in range(5)]
    second = [pltpu.make_async_copy(held[i], outs[i], sems.at[i]) for i in range(5)]
    for copy in first:
        copy.start()
    for a, b in zip(first, second):
        a.wait()
        b.start()
    for copy in second:
        copy.wait()


def shards(q, kp, vp, kr, vr, do, lengths, assign):
    bf, f32 = jnp.bfloat16, jnp.float32
    dma = pltpu.SemaphoreType.DMA
    hbm = pl.BlockSpec(memory_space=pl.ANY)
    smem = pl.BlockSpec(memory_space=pltpu.SMEM)
    H = HEADS
    outs = pl.pallas_call(
        kernel,
        out_shape=(
            jax.ShapeDtypeStruct(q.shape, bf),
            jax.ShapeDtypeStruct(kp.shape, bf),
            jax.ShapeDtypeStruct(vp.shape, bf),
            jax.ShapeDtypeStruct(kr.shape, bf),
            jax.ShapeDtypeStruct(vr.shape, bf),
        ),
        in_specs=[hbm] * 6 + [smem] * 2,
        out_specs=(hbm,) * 5,
        scratch_shapes=[
            pltpu.VMEM((ROWS, H * GROUP * DIM), bf),
            pltpu.VMEM((ROWS, H * GROUP * DIM), bf),
            pltpu.VMEM((H, DIM, GROUP * ROWS), bf),
            pltpu.VMEM((H, DIM, GROUP * ROWS), bf),
            pltpu.VMEM((H, 2, PREFIX, DIM), bf),
            pltpu.VMEM((H, 2, 3, 4, ROWS, DIM), bf),
            pltpu.VMEM((WINDOW, ROWS), f32),
            pltpu.VMEM((1, ROWS), f32),
            pltpu.VMEM((KEYS, QB), f32),
            pltpu.VMEM((KEYS, QB), f32),
            pltpu.VMEM((KEYS, GROUP * ROWS), bf),
            pltpu.VMEM((H, KEYS, GROUP * ROWS), bf),
            pltpu.VMEM((H, 2, KEPT, DIM), f32),
            pltpu.VMEM((H, DIM, KEYS), bf),
            pltpu.VMEM((H, 3, 4, 2, ROWS, DIM), bf),
            pltpu.VMEM((H, 3, 2, 2, ROWS, DIM), bf),
            pltpu.VMEM((H, 2, 2, ROWS, DIM), bf),
            pltpu.VMEM((H, 2, 2, ROWS, DIM), bf),
            pltpu.VMEM((H, PREFIX, DIM), bf),
            pltpu.VMEM((H, PREFIX, DIM), bf),
            pltpu.VMEM((H, SIDE, 256, DIM), bf),
            pltpu.VMEM((H, 3, 256, DIM), bf),
            pltpu.VMEM((H, SIDE, 64, DIM), bf),
            pltpu.VMEM((H, SIDE, 64, DIM), f32),
            pltpu.VMEM((H, 3, 64, DIM), bf),
            pltpu.VMEM((H, SIDE, 16, DIM), f32),
            pltpu.VMEM((H, 3, 16, DIM), f32),
            pltpu.VMEM((8, H, 16, DIM), bf),
            pltpu.VMEM((2, H, ROWS, DIM), bf),
            pltpu.VMEM((2, 64, H * DIM), bf),
            dma((14,)),
            dma((H, 2)), dma((H, 2)), dma((H, 3)), dma((H, 3)),
            dma((2, 3)), dma((2, 3)), dma((2, 3)), dma((2, 3)),
            dma((H, 3)), dma((H, 3)), dma((H,)), dma((H,)),
            dma((H, 3)), dma((H, 3)), dma((H, 2)), dma((H, 2)),
            dma((H,)), dma((H,)), dma((H, 3)), dma((H, 3)),
            dma((H, 3)), dma((H, 3)), dma((H, 3)), dma((H, 3)),
            dma((7,)), dma((7,)),
        ],
        compiler_params=pltpu.CompilerParams(
            collective_id=0, has_side_effects=True, vmem_limit_bytes=63 * 1024 * 1024
        ),
        name="attention_backward",
    )(q, kp, vp, kr, vr, do, lengths, assign)
    return pl.pallas_call(
        hand_over,
        out_shape=tuple(jax.ShapeDtypeStruct(o.shape, o.dtype) for o in outs),
        in_specs=[hbm] * 5,
        out_specs=(hbm,) * 5,
        scratch_shapes=[pltpu.VMEM(o.shape, o.dtype) for o in outs] + [dma((5,))],
        compiler_params=pltpu.CompilerParams(vmem_limit_bytes=63 * 1024 * 1024),
        name="hand_over",
    )(*outs)


def solution(mesh):
    rows = P(("dp", "smp"), "ctx", None)
    prefix = P(("dp", "ctx"), None)
    return jax.shard_map(
        shards,
        mesh=mesh,
        in_specs=(rows, prefix, prefix, rows, rows, rows, P("dp"), P("dp")),
        out_specs=(rows, prefix, prefix, rows, rows),
        check_vma=False,
    )
```
